256 devices in a mesh: tm: 64 (over z_hi, y, x), space: 4 (over z_lo, core).
Axes of the slice: x: 4, y: 4, z: 8 (z_hi: 4, z_lo: 2; z = z_hi * 2 + z_lo), core: 2. Of those that a mesh axis runs over, the one named last changes fastest.
Arguments:
- node_fields: float32 [64, 5, 32, 128, 128], P('tm', None, 'space'), may hold values from -6 to 6
- region_label: int32 [32, 128, 128], P('space'), may hold values from 0 to 3
- sheet_shift: int32 [64, 128], P('tm'), may hold values from 0 to 1
- diffusivity: float32 [4], replicated, may hold values from 0.02 to 0.15
Outputs:
- updated_nodes: float32 [64, 5, 32, 128, 128], P('tm', None, 'space')
The draws below stay inside these ranges and needn't reach their ends.
All inputs are finite; a program needn't handle non-finite values.
Results may differ from the reference program's by a relative error of at most 0.00002.
Values sent between devices are 32-bit elements; how exact they have to be, the bound alone decides.
No kernel may reach another device: no remote copies, remote signals or barrier semaphores. Data moves between devices by JAX's collectives and lax.ppermute only.
A program may use at most 64 MiB of HBM per device.

```python
import math
import jax
import jax.numpy as jnp
import numpy as np
from jax import lax

NX = 128
NY = 128
NODES = 5
REGIONS = 4
FINE_SWEEPS = 2
SLICES = 64
NZ = 32


def touch_ends(values, key, low, largest):
    dims = values.shape
    spot = [jax.random.randint(jax.random.fold_in(key, axis), (), 0, dims[axis]) for axis in range(len(dims))]
    values = values.at[tuple(spot)].set(low)
    longest = dims.index(max(dims))
    spot[longest] = (spot[longest] + 1) % dims[longest]
    return values.at[tuple(spot)].set(largest)


def level_of(rng, dims, cuts, low, top_value):
    gain, own = 1.0, jax.random.fold_in(rng, 6)
    for axis_at, blocks in cuts:
        steps = jnp.exp(jax.random.uniform(jax.random.fold_in(own, axis_at), (blocks,), jnp.float32, low / len(cuts), top_value / len(cuts)))
        gain = gain * jnp.repeat(steps, dims[axis_at] // blocks).reshape([-1 if axis == axis_at else 1 for axis in range(len(dims))])
    return gain


def gaussian(own_key, dims, scale, bound, shards=(), dtype=jnp.bfloat16):
    drawn = jax.random.normal(own_key, dims, jnp.float32) * scale
    if len(shards) > 0:
        drawn = level_of(own_key, dims, shards, -0.22, 0.18) * drawn
    return jnp.clip(drawn, min=-bound, max=bound).astype(dtype)


def setup_inputs(seed: int = 0) -> dict:
    arg_keys = jax.random.split(jax.random.key(seed), 5)
    node_fields = gaussian(arg_keys[0], (SLICES, NODES, NZ, NX, NY), 1.0, 6.0, ((0, 64), (2, 4)), jnp.float32)
    region_label = touch_ends(jax.random.randint(arg_keys[1], (NZ, NX, NY), 0, REGIONS), jax.random.fold_in(arg_keys[1], 1), 0, REGIONS - 1).astype(jnp.int32)
    sheet_shift = touch_ends(jax.random.randint(arg_keys[2], (SLICES, NY), 0, 2), jax.random.fold_in(arg_keys[2], 1), 0, 1).astype(jnp.int32)
    diffusivity = jnp.clip(jnp.exp(jax.random.uniform(arg_keys[3], (REGIONS,), jnp.float32, math.log(0.02), math.log(0.15))), 0.02, 0.15)
    return dict(node_fields=node_fields, region_label=region_label, sheet_shift=sheet_shift, diffusivity=diffusivity)


slice_length = 1.0

def node_tables():
    radius = math.sqrt(3.0 / 7.0)
    points = [0.0, (1.0 - radius) / 2.0, 0.5, (1.0 + radius) / 2.0, 1.0]
    integrals = np.zeros((4, 5))
    for column in range(5):
        coeffs = [1.0]
        divisor = 1.0
        for other in range(5):
            if other != column:
                anchor = points[other]
                product = [0.0] * (len(coeffs) + 1)
                for degree in range(len(coeffs)):
                    product[degree + 1] = product[degree + 1] + coeffs[degree]
                    product[degree] = product[degree] - anchor * coeffs[degree]
                coeffs = product
                divisor = divisor * (points[column] - anchor)
        for row in range(4):
            bottom = points[row]
            summit = points[row + 1]
            amount = 0.0
            for degree in range(len(coeffs)):
                amount = amount + coeffs[degree] / (degree + 1) * (summit ** (degree + 1) - bottom ** (degree + 1))
            integrals[row, column] = amount / divisor
    return (np.array(points), integrals)

def combine(coefficients, stack):
    total = float(coefficients[0]) * stack[0]
    for index in range(1, len(coefficients)):
        total = total + float(coefficients[index]) * stack[index]
    return total

def lookup(labels, table):
    result = jnp.zeros(labels.shape, jnp.float32)
    for region in range(table.shape[0]):
        result = result + jnp.where(labels == region, table[region], 0.0)
    return result

def restrict(field):
    shape = field.shape
    blocks = field.reshape(shape[:-3] + (shape[-3] // 4, 4, shape[-2] // 2, 2, shape[-1]))
    return lax.optimization_barrier(jnp.mean(blocks, axis=(-4, -2)))

def prolong(coarse):
    return jnp.repeat(jnp.repeat(coarse, 4, axis=-3), 2, axis=-2)

def pad_rows(field):
    return jnp.pad(field, [(0, 0)] * (field.ndim - 3) + [(1, 1), (0, 0), (0, 0)])

def neighbours(padded):
    center = padded[..., 1:-1, :, :]
    vertical = padded[..., 2:, :, :] + padded[..., :-2, :, :]
    across = jnp.roll(center, 1, -2) + jnp.roll(center, -1, -2)
    sideways = jnp.pad(center, [(0, 0)] * (center.ndim - 1) + [(1, 1)])
    lateral = sideways[..., 2:] + sideways[..., :-2]
    return (center, vertical, across, lateral)

def fine_rate(padded, kappa, advect):
    center, vertical, across, lateral = neighbours(padded)
    diffusion = kappa * (vertical + across + lateral - 6.0 * center)
    return diffusion - advect * (center - jnp.roll(center, 1, -2))

def coarse_rate(padded, kappa, advect):
    center, vertical, across, lateral = neighbours(padded)
    diffusion = kappa * ((vertical - 2.0 * center) / 16.0 + (across - 2.0 * center) / 4.0 + (lateral - 2.0 * center))
    return diffusion - 0.5 * advect * (center - jnp.roll(center, 1, -2))

def coarse_advance(initial, padded, kappa, advect, constant):
    return initial + slice_length * coarse_rate(padded, kappa, advect) + constant

def apply_correction(fields, delta_start, delta_end):
    times_table, integral_table = node_tables()
    pieces = []
    for node in range(NODES):
        weight = float(times_table[node])
        pieces.append(fields[node] + prolong((1.0 - weight) * delta_start + weight * delta_end))
    return jnp.stack(pieces)

def fine_sweeps(corrected, rates, kappa, advect, rims):
    times_table, integral_table = node_tables()
    old_values, old_rates = (corrected, rates)
    for sweep in range(FINE_SWEEPS):
        values = [old_values[0]]
        new_rates = [old_rates[0]]
        for node in range(NODES - 1):
            spacing = float(times_table[node + 1] - times_table[node]) * slice_length
            value = values[node] + spacing * (new_rates[node] - old_rates[node]) + slice_length * combine(integral_table[node], old_rates)
            values.append(value)
            if node < NODES - 2 or sweep < FINE_SWEEPS - 1:
                new_rates.append(fine_rate(rims(value[None]), kappa, advect)[0])
        old_values = jnp.stack(values)
        if sweep < FINE_SWEEPS - 1:
            old_rates = jnp.stack(new_rates)
    return old_values

def reference(node_fields, region_label, sheet_shift, diffusivity):
    times_table, integral_table = node_tables()
    weight_table = integral_table.sum(axis=0)
    kappa = lookup(region_label, diffusivity)
    kappa_coarse = restrict(kappa)
    advects = sheet_shift.astype(jnp.float32) / slice_length
    previous = jnp.concatenate([node_fields[0:1, 0], node_fields[:-1, NODES - 1]], 0)

    def prepare(inputs):
        fields, start, advect = inputs
        fields = jnp.concatenate([start[None], fields[1:]], 0)
        rates = fine_rate(pad_rows(fields), kappa, advect)
        coarse_start = restrict(start)
        moved = restrict(slice_length * combine(weight_table, rates))
        constant = moved - slice_length * coarse_rate(pad_rows(coarse_start), kappa_coarse, advect)
        return (coarse_start, constant)
    coarse_starts, constants = lax.map(prepare, (node_fields, previous, advects))

    def chain(carry, inputs):
        constant, advect = inputs
        ending = coarse_advance(carry, pad_rows(carry), kappa_coarse, advect, constant)
        return (ending, (carry, ending))
    finished, (begins, endings) = lax.scan(chain, coarse_starts[0], (constants, advects))

    def finish(inputs):
        fields, start, advect, begin, ending, coarse_start = inputs
        fields = jnp.concatenate([start[None], fields[1:]], 0)
        corrected = apply_correction(fields, begin - coarse_start, ending - restrict(fields[NODES - 1]))
        rates = fine_rate(pad_rows(corrected), kappa, advect)
        return fine_sweeps(corrected, rates, kappa, advect, pad_rows)
    return lax.map(finish, (node_fields, previous, advects, begins, endings, coarse_starts))
```

```python
import functools
import math

import jax
import jax.numpy as jnp
import numpy as np
from jax import lax
from jax.experimental import pallas as pl
from jax.experimental.pallas import tpu as pltpu
from jax.sharding import Mesh
from jax.sharding import PartitionSpec as P

NODES = 5
STEPS = NODES - 1
F32 = jnp.float32
TM = ("zh", "y", "x")
MIB = 1 << 20


def node_tables():
    radius = math.sqrt(3.0 / 7.0)
    points = [0.0, (1.0 - radius) / 2.0, 0.5, (1.0 + radius) / 2.0, 1.0]
    integrals = np.zeros((4, 5))
    for column in range(5):
        coeffs = [1.0]
        divisor = 1.0
        for other in range(5):
            if other != column:
                anchor = points[other]
                product = [0.0] * (len(coeffs) + 1)
                for degree in range(len(coeffs)):
                    product[degree + 1] = product[degree + 1] + coeffs[degree]
                    product[degree] = product[degree] - anchor * coeffs[degree]
                coeffs = product
                divisor = divisor * (points[column] - anchor)
        for row in range(4):
            bottom = points[row]
            summit = points[row + 1]
            amount = 0.0
            for degree in range(len(coeffs)):
                amount = amount + coeffs[degree] / (degree + 1) * (
                    summit ** (degree + 1) - bottom ** (degree + 1)
                )
            integrals[row, column] = amount / divisor
    return (np.array(points), integrals)


TAU, Q = node_tables()
WEIGHTS = Q.sum(axis=0)
DT = TAU[1:] - TAU[:-1]


def kappa_of(labels, table):
    value = jnp.where(labels == 3, table[3], 0.0)
    for region in range(3):
        value = jnp.where(labels == region, table[region], value)
    return value


def rate(below, mid, above, kappa, advect):
    rows, cols = mid.shape
    lane = lax.broadcasted_iota(jnp.int32, (1, cols), 1)
    behind = pltpu.roll(mid, 1, 0)
    ahead = pltpu.roll(mid, rows - 1, 0)
    left = jnp.where(lane == 0, 0.0, pltpu.roll(mid, 1, 1))
    right = jnp.where(lane == cols - 1, 0.0, pltpu.roll(mid, cols - 1, 1))
    total = ((below + above) + (behind + ahead)) + (left + right)
    return kappa * (total - 6.0 * mid) - advect * (mid - behind)


def sums_kernel(info, nodes, sums, weighted):
    first = (info[0] == 0).astype(F32)
    for z in range(nodes.shape[2]):
        u = [nodes[0, j, z] for j in range(1, NODES)]
        for m in range(STEPS):
            coef = [float(Q[m, j]) for j in range(1, NODES)]
            if m > 0:
                coef[m - 1] -= float(DT[m])
            total = coef[0] * u[0]
            for j in range(1, STEPS):
                total = total + coef[j] * u[j]
            sums[m, z] = total
        total = float(WEIGHTS[1]) * u[0]
        for j in range(1, STEPS):
            total = total + float(WEIGHTS[j + 1]) * u[j]
        weighted[z] = total + (first * float(WEIGHTS[0])) * nodes[0, 0, z]


def node_sums(info, node_fields):
    _, _, nz, nx, ny = node_fields.shape
    cut = 2
    return pl.pallas_call(
        sums_kernel,
        grid_spec=pltpu.PrefetchScalarGridSpec(
            num_scalar_prefetch=1,
            grid=(nz // cut,),
            in_specs=[pl.BlockSpec((1, NODES, cut, nx, ny), lambda i, *_: (0, 0, i, 0, 0))],
            out_specs=[
                pl.BlockSpec((STEPS, cut, nx, ny), lambda i, *_: (0, i, 0, 0)),
                pl.BlockSpec((cut, nx, ny), lambda i, *_: (i, 0, 0)),
            ],
        ),
        out_shape=[
            jax.ShapeDtypeStruct((STEPS, nz, nx, ny), F32),
            jax.ShapeDtypeStruct((nz, nx, ny), F32),
        ],
        compiler_params=pltpu.CompilerParams(vmem_limit_bytes=16 * MIB),
        cost_estimate=pl.CostEstimate(flops=10_000_000, bytes_accessed=6_000_000, transcendentals=0),
        name="node_sums",
    )(info, node_fields)


def residual_kernel(
    info, table, weighted, arrived, u0, u4, labels, shift, w_low, w_high, s_low, s_high,
    coarse, start, wide, block,
):
    nz, nx, ny = weighted.shape
    first = info[0] == 0
    advect = shift[...].astype(F32)
    w0 = float(WEIGHTS[0])
    for z in range(nz):
        wide[z + 1] = weighted[z] + w0 * arrived[z]
    wide[0] = w_low[0] + w0 * s_low[0]
    wide[nz + 1] = w_high[0] + w0 * s_high[0]
    for zb in range(nz // 4):
        total = None
        ksum = None
        for k in range(4):
            z = 4 * zb + k
            kappa = kappa_of(labels[z], table)
            begin = jnp.where(first, u0[0, 0, z], arrived[z])
            start[z] = begin
            value = begin - u4[0, 0, z] + rate(wide[z], wide[z + 1], wide[z + 2], kappa, advect)
            total = value if total is None else total + value
            ksum = kappa if ksum is None else ksum + kappa
        block[0] = total
        block[1] = ksum
        for f in range(2):
            even = block[f, pl.ds(0, nx // 2, stride=2), :]
            odd = block[f, pl.ds(1, nx // 2, stride=2), :]
            coarse[f, zb] = (even + odd) * 0.125


def residual(info, table, weighted, arrived, node_fields, labels, shift, w_low, w_high, s_low, s_high):
    nz, nx, ny = weighted.shape
    full = pl.BlockSpec(memory_space=pltpu.VMEM)
    smem = pl.BlockSpec(memory_space=pltpu.SMEM)

    def node(j):
        return pl.BlockSpec((1, 1, nz, nx, ny), lambda i: (0, j, 0, 0, 0))

    def whole(shape):
        return pl.BlockSpec(shape, lambda i: (0,) * len(shape))

    return pl.pallas_call(
        residual_kernel,
        grid=(1,),
        in_specs=[
            smem, smem, whole((nz, nx, ny)), whole((nz, nx, ny)), node(0), node(NODES - 1),
            whole((nz, nx, ny)), whole((1, ny)),
            whole((1, nx, ny)), whole((1, nx, ny)), whole((1, nx, ny)), whole((1, nx, ny)),
        ],
        out_specs=[whole((2, nz // 4, nx // 2, ny)), whole((nz, nx, ny))],
        out_shape=[
            jax.ShapeDtypeStruct((2, nz // 4, nx // 2, ny), F32),
            jax.ShapeDtypeStruct((nz, nx, ny), F32),
        ],
        scratch_shapes=[pltpu.VMEM((nz + 2, nx, ny), F32), pltpu.VMEM((2, nx, ny), F32)],
        compiler_params=pltpu.CompilerParams(vmem_limit_bytes=16 * MIB),
        cost_estimate=pl.CostEstimate(flops=4_000_000, bytes_accessed=4_000_000, transcendentals=0),
        name="residual",
    )(info, table, weighted, arrived, node_fields, node_fields, labels, shift, w_low, w_high, s_low, s_high)


def coarse_step(src, dst, kappa, half):
    nx, nz, ny = kappa.shape
    lane = lax.broadcasted_iota(jnp.int32, (nz, ny), 1)
    sub = lax.broadcasted_iota(jnp.int32, (nz, ny), 0)
    past, mid = src[nx - 1], src[0]
    for x in range(nx):
        ahead = src[(x + 1) % nx]
        below = jnp.where(sub == 0, 0.0, pltpu.roll(mid, 1, 0))
        above = jnp.where(sub == nz - 1, 0.0, pltpu.roll(mid, nz - 1, 0))
        left = jnp.where(lane == 0, 0.0, pltpu.roll(mid, 1, 1))
        right = jnp.where(lane == ny - 1, 0.0, pltpu.roll(mid, ny - 1, 1))
        total = (below + above) * 0.0625 + (past + ahead) * 0.25 + ((left + right) - 2.625 * mid)
        dst[x] = mid + kappa[x] * total - half * (mid - past)
        past, mid = mid, ahead


def entry_kernel(info, gathered, shift, field, kappa, packet):
    ns, _, nzs, nx, ny = gathered.shape
    rows = nx // 2
    for z in range(ns * nzs):
        field[:, z, :] = gathered[z // nzs, 0, z % nzs]
        kappa[:, z, :] = gathered[z // nzs, 1, z % nzs]
    core = info[4] % 2
    packet[pl.ds(0, rows)] = field[pl.ds(core * rows, rows)]
    packet[rows] = jnp.broadcast_to(shift[...].astype(F32) * 0.5, packet.shape[1:])


def chain_entry(info, gathered, shift):
    ns, _, nzs, nx, ny = gathered.shape
    nz = ns * nzs
    vmem = pl.BlockSpec(memory_space=pltpu.VMEM)
    return pl.pallas_call(
        entry_kernel,
        in_specs=[pl.BlockSpec(memory_space=pltpu.SMEM), vmem, vmem],
        out_specs=[vmem] * 3,
        out_shape=[
            jax.ShapeDtypeStruct((nx, nz, ny), F32),
            jax.ShapeDtypeStruct((nx, nz, ny), F32),
            jax.ShapeDtypeStruct((nx // 2 + 1, nz, ny), F32),
        ],
        compiler_params=pltpu.CompilerParams(vmem_limit_bytes=8 * MIB),
        name="chain_entry",
    )(info, gathered, shift)


def place(members, slot, core, mine, theirs, rows):
    members[slot, pl.ds(core * rows, rows)] = mine[pl.ds(0, rows)]
    members[slot, pl.ds((1 - core) * rows, rows)] = theirs[pl.ds(0, rows)]


def level_kernel(length, axis, info, own, own_tail, before, kappa, *refs):
    packets, (packet, after, members, halves, work, saved) = refs[:6], refs[6:]
    nx, nz, ny = kappa.shape
    rows = nx // 2
    core, position = info[4] % 2, info[axis]
    inner = info[3] if length > 1 else 0
    members[position] = own[...]
    for j in range(length):
        halves[position * length + j] = jnp.broadcast_to(own_tail[j : j + 1], (nz, ny))
    for k in range(1, 4):
        slot = (position + (4 - k)) % 4
        mine, theirs = packets[2 * (k - 1)], packets[2 * (k - 1) + 1]
        place(members, slot, core, mine, theirs, rows)
        for j in range(length):
            halves[slot * length + j] = jnp.broadcast_to(mine[rows, j : j + 1], (nz, ny))
    work[0] = members[0]
    saved[...] = jnp.zeros(saved.shape, F32)

    def turn(t, _):
        group, inside = t // length, t % length
        here, there = (t - length) % 2, (t - length + 1) % 2

        @pl.when((group == position) & (inside == inner))
        def _():
            saved[...] = work[here]

        coarse_step(work.at[here], work.at[there], kappa, halves[t])

        @pl.when(inside == length - 1)
        def _():
            work[there] = work[there] + members[group]

        return 0

    lax.fori_loop(length, 4 * length, turn, 0)
    last = (3 * length) % 2
    after[...] = saved[...] + before[...] if length > 1 else saved[...]
    if length > 1:
        packet[pl.ds(0, rows)] = work[last, pl.ds(core * rows, rows)]
        for j in range(4 * length):
            packet[rows + j // 8, j % 8 : j % 8 + 1] = halves[j, 0:1]
    else:
        packet[pl.ds(0, nx)] = work[last]
        for j in range(4):
            packet[nx, j : j + 1] = halves[j, 0:1]


def chain_level(length, axis, info, own, own_tail, before, kappa, packets):
    nx, nz, ny = kappa.shape
    rows = nx // 2
    vmem = pl.BlockSpec(memory_space=pltpu.VMEM)
    size = rows + 2 if length > 1 else nx + 1
    return pl.pallas_call(
        functools.partial(level_kernel, length, axis),
        in_specs=[pl.BlockSpec(memory_space=pltpu.SMEM)] + [vmem] * (4 + len(packets)),
        out_specs=[vmem] * 2,
        out_shape=[
            jax.ShapeDtypeStruct((size, nz, ny), F32),
            jax.ShapeDtypeStruct((nx, nz, ny), F32),
        ],
        scratch_shapes=[
            pltpu.VMEM((4, nx, nz, ny), F32),
            pltpu.VMEM((4 * length, nz, ny), F32),
            pltpu.VMEM((2, nx, nz, ny), F32),
            pltpu.VMEM((nx, nz, ny), F32),
        ],
        compiler_params=pltpu.CompilerParams(vmem_limit_bytes=12 * MIB),
        name=f"chain_level_{length}",
    )(info, own, own_tail, before, kappa, *packets)


def final_kernel(info, field, before, kappa, tail, *refs):
    packets, (coarse, members, halves, work) = refs[:6], refs[6:]
    nx, nz, ny = kappa.shape
    rows = nx // 2
    core, zh = info[4] % 2, info[1]
    inside = info[2] * 4 + info[3]
    for j in range(16):
        halves[zh * 16 + j] = jnp.broadcast_to(tail[j // 8, j % 8 : j % 8 + 1], (nz, ny))
    for k in range(1, 4):
        slot = (zh + (4 - k)) % 4
        mine, theirs = packets[2 * (k - 1)], packets[2 * (k - 1) + 1]
        place(members, slot, core, mine, theirs, rows)
        for j in range(16):
            halves[slot * 16 + j] = jnp.broadcast_to(mine[rows + j // 8, j % 8 : j % 8 + 1], (nz, ny))
    begin = zh * 16
    work[0] = jnp.where(zh > 0, members[0], 0.0)
    low = jnp.where(zh > 0, 16, 0)
    high = jnp.where(zh > 0, begin + inside, 0)

    def turn(t, _):
        here, there = t % 2, (t + 1) % 2
        coarse_step(work.at[here], work.at[there], kappa, halves[t])

        @pl.when((t % 16 == 15) & (t < begin))
        def _():
            work[there] = work[there] + members[t // 16]

        return 0

    lax.fori_loop(low, high, turn, 0)
    here, there = high % 2, (high + 1) % 2
    work[here] = work[here] + before[...]
    coarse_step(work.at[here], work.at[there], kappa, halves[begin + inside])
    members[0] = work[here]
    members[1] = work[there] + field[...] - work[here]
    blank = jnp.zeros((nx, ny), F32)
    for f in range(2):
        for edge in range(2):
            coarse[f, edge] = blank
            coarse[f, nz + 2 + edge] = blank
        for z in range(nz):
            coarse[f, z + 2] = members[f, :, z, :]


def chain_final(info, field, before, kappa, tail, packets):
    nx, nz, ny = kappa.shape
    vmem = pl.BlockSpec(memory_space=pltpu.VMEM)
    return pl.pallas_call(
        final_kernel,
        in_specs=[pl.BlockSpec(memory_space=pltpu.SMEM)] + [vmem] * (4 + len(packets)),
        out_specs=vmem,
        out_shape=jax.ShapeDtypeStruct((2, nz + 4, nx, ny), F32),
        scratch_shapes=[
            pltpu.VMEM((4, nx, nz, ny), F32),
            pltpu.VMEM((64, nz, ny), F32),
            pltpu.VMEM((2, nx, nz, ny), F32),
        ],
        compiler_params=pltpu.CompilerParams(vmem_limit_bytes=12 * MIB),
        name="chain_final",
    )(info, field, before, kappa, tail, *packets)


def sweeps_kernel(
    info, table, coarse, sums, sums_low, sums_high, start, start_low, start_high,
    labels, labels_low, labels_high, shift, out,
    lift, kappa, first, fields, second, mixed,
):
    nz, nx, ny = start.shape
    wide = 3 * nz
    space = info[4]
    advect = shift[...].astype(F32)
    for f in range(2):
        for k in range(wide // 4):
            value = coarse[f, space * (nz // 4) + k]
            lift[f, k, pl.ds(0, nx // 2, stride=2), :] = value
            lift[f, k, pl.ds(1, nx // 2, stride=2), :] = value

    def parts(body, low, high):
        lax.fori_loop(low, high, lambda z, _: (body(z), 0)[1], 0)

    inside_low, inside_high = space > 0, space < 3
    for base, ref, keep in (
        (0, labels_low, inside_low), (nz, labels, None), (2 * nz, labels_high, inside_high),
    ):
        def fill(z, base=base, ref=ref, keep=keep):
            value = kappa_of(ref[z], table)
            kappa[base + z] = value if keep is None else jnp.where(keep, value, 0.0)
        parts(fill, 0, nz)

    q00 = float(Q[0, 0])
    for base, ref, src in (
        (0, start_low, sums_low), (nz, start, sums), (2 * nz, start_high, sums_high),
    ):
        def opening(z, base=base, ref=ref, src=src):
            at = (base + z) // 4
            begin, grow = lift[0, at], lift[1, at]
            own = ref[z]
            first[base + z] = own + begin
            mixed[base + z] = (
                src[0, z] + q00 * own + float(DT[0]) * begin + float(0.5 * DT[0] ** 2) * grow
            )
        parts(opening, 0, nz)

    def advance(source, target, low, high):
        def body(z):
            target[z] = source[z] + rate(mixed[z - 1], mixed[z], mixed[z + 1], kappa[z], advect)
        parts(body, low, high)

    advance(first, fields.at[0], 1, wide - 1)
    for m in range(1, STEPS):
        for base, ref, src in (
            (0, start_low, sums_low), (nz, start, sums), (2 * nz, start_high, sums_high),
        ):
            def mixing(z, base=base, ref=ref, src=src, m=m):
                at = (base + z) // 4
                mixed[base + z] = (
                    float(DT[m]) * fields[m - 1, base + z]
                    + src[m, z]
                    + float(Q[m, 0]) * ref[z]
                    + float(0.5 * DT[m] ** 2) * lift[1, at]
                )
            parts(mixing, m if base == 0 else 0, nz - m if base == 2 * nz else nz)
        advance(fields.at[m - 1], fields.at[m], m + 1, wide - 1 - m)

    for m in range(STEPS):
        edge = STEPS + m

        def mixing(z, m=m):
            total = float(Q[m, 0] - (DT[0] if m == 0 else 0.0)) * first[z]
            for j in range(1, NODES):
                total = total + float(Q[m, j] - (DT[m] if m == j else 0.0)) * fields[j - 1, z]
            before = first[z] if m == 0 else second[m - 1, z]
            mixed[z] = total + float(DT[m]) * before

        parts(mixing, edge, wide - edge)
        advance(first if m == 0 else second.at[m - 1], second.at[m], edge + 1, wide - edge - 1)

    def emit(z):
        out[0, 0, z] = first[nz + z]
        for m in range(STEPS):
            out[0, m + 1, z] = second[m, nz + z]
    parts(emit, 0, nz)


def fine_sweeps(info, table, coarse, sums, sums_low, sums_high, start, start_low, start_high,
                labels, labels_low, labels_high, shift):
    nz, nx, ny = start.shape
    vmem = pl.BlockSpec(memory_space=pltpu.VMEM)
    smem = pl.BlockSpec(memory_space=pltpu.SMEM)
    wide = 3 * nz
    return pl.pallas_call(
        sweeps_kernel,
        in_specs=[smem, smem] + [vmem] * 11,
        out_specs=vmem,
        out_shape=jax.ShapeDtypeStruct((1, NODES, nz, nx, ny), F32),
        scratch_shapes=[
            pltpu.VMEM((2, wide // 4, nx, ny), F32),
            pltpu.VMEM((wide, nx, ny), F32),
            pltpu.VMEM((wide, nx, ny), F32),
            pltpu.VMEM((STEPS, wide, nx, ny), F32),
            pltpu.VMEM((STEPS, wide, nx, ny), F32),
            pltpu.VMEM((wide, nx, ny), F32),
        ],
        compiler_params=pltpu.CompilerParams(vmem_limit_bytes=48 * MIB),
        name="fine_sweeps",
    )(info, table, coarse, sums, sums_low, sums_high, start, start_low, start_high,
      labels, labels_low, labels_high, shift)


def to_space(value, by):
    return lax.ppermute(value, "space", [(i, i + by) for i in range(4) if 0 <= i + by < 4])


def to_next(value, by):
    axes = TM + ("space",)
    pairs = [
        (4 * n + s, 4 * (n + 1) + s + by) for n in range(63) for s in range(4) if 0 <= s + by < 4
    ]
    return lax.ppermute(value, axes, pairs)


def swap_core(value):
    return lax.ppermute(value, "space", [(0, 1), (1, 0), (2, 3), (3, 2)])


def gather_axis(packet, axis):
    packets = []
    for k in range(1, 4):
        got = lax.ppermute(packet, axis, [(i, (i + k) % 4) for i in range(4)])
        packets += [got, swap_core(got)]
    return packets


def shards(node_fields, region_label, sheet_shift, diffusivity):
    zh, y, x = (lax.axis_index(a) for a in TM)
    space = lax.axis_index("space")
    info = jnp.stack([zh * 16 + y * 4 + x, zh, y, x, space]).astype(jnp.int32)
    nz = region_label.shape[0]
    last = node_fields[0, NODES - 1]
    arrived = to_next(last, 0)
    s_low = to_next(last[nz - 1 :], 1)
    s_high = to_next(last[:1], -1)
    sums, weighted = node_sums(info, node_fields)
    w_low = to_space(weighted[nz - 1 :], 1)
    w_high = to_space(weighted[:1], -1)
    coarse, start = residual(
        info, diffusivity, weighted, arrived, node_fields, region_label, sheet_shift,
        w_low, w_high, s_low, s_high,
    )
    sums_low, sums_high = to_space(sums, 1), to_space(sums, -1)
    labels_low, labels_high = to_space(region_label, 1), to_space(region_label, -1)
    start_low, start_high = to_space(start, 1), to_space(start, -1)

    gathered = lax.all_gather(coarse, "space", axis=0, tiled=False)
    field, kappa, packet = chain_entry(info, gathered, sheet_shift)
    rows = field.shape[0] // 2
    packets = gather_axis(packet, "x")
    one, prefix = chain_level(1, 3, info, field, packet[rows], field, kappa, packets)
    own = one[: 2 * rows]
    half = lax.dynamic_slice_in_dim(own, (space % 2) * rows, rows, 0)
    packet = jnp.concatenate([half, one[2 * rows :]], 0)
    packets = gather_axis(packet, "y")
    two, prefix = chain_level(4, 2, info, own, one[2 * rows], prefix, kappa, packets)
    packets = gather_axis(two, "zh")
    correction = chain_final(info, field, prefix, kappa, two[rows:], packets)
    return fine_sweeps(
        info, diffusivity, correction, sums, sums_low, sums_high, start, start_low, start_high,
        region_label, labels_low, labels_high, sheet_shift,
    )


def solution(mesh):
    grid = Mesh(mesh.devices.reshape(4, 4, 4, 4), TM + ("space",))
    in_specs = (P(TM, None, "space", None, None), P("space", None, None), P(TM, None), P())
    out_specs = P(TM, None, "space", None, None)
    return jax.shard_map(shards, mesh=grid, in_specs=in_specs, out_specs=out_specs, check_vma=False)
```

```python
import functools
import math

import jax
import jax.numpy as jnp
import numpy as np
from jax import lax
from jax.experimental import pallas as pl
from jax.experimental.pallas import tpu as pltpu
from jax.sharding import Mesh
from jax.sharding import PartitionSpec as P

NODES = 5
STEPS = NODES - 1
F32 = jnp.float32
TM = ("zh", "y", "x")
MIB = 1 << 20


def node_tables():
    radius = math.sqrt(3.0 / 7.0)
    points = [0.0, (1.0 - radius) / 2.0, 0.5, (1.0 + radius) / 2.0, 1.0]
    integrals = np.zeros((4, 5))
    for column in range(5):
        coeffs = [1.0]
        divisor = 1.0
        for other in range(5):
            if other != column:
                anchor = points[other]
                product = [0.0] * (len(coeffs) + 1)
                for degree in range(len(coeffs)):
                    product[degree + 1] = product[degree + 1] + coeffs[degree]
                    product[degree] = product[degree] - anchor * coeffs[degree]
                coeffs = product
                divisor = divisor * (points[column] - anchor)
        for row in range(4):
            bottom = points[row]
            summit = points[row + 1]
            amount = 0.0
            for degree in range(len(coeffs)):
                amount = amount + coeffs[degree] / (degree + 1) * (
                    summit ** (degree + 1) - bottom ** (degree + 1)
                )
            integrals[row, column] = amount / divisor
    return (np.array(points), integrals)


TAU, Q = node_tables()
WEIGHTS = Q.sum(axis=0)
DT = TAU[1:] - TAU[:-1]


def kappa_of(labels, table):
    value = jnp.where(labels == 3, table[3], 0.0)
    for region in range(3):
        value = jnp.where(labels == region, table[region], value)
    return value


def rate(below, mid, above, behind, ahead, kappa, advect):
    cols = mid.shape[1]
    lane = lax.broadcasted_iota(jnp.int32, mid.shape, 1)
    left = jnp.where(lane == 0, 0.0, pltpu.roll(mid, 1, 1))
    right = jnp.where(lane == cols - 1, 0.0, pltpu.roll(mid, cols - 1, 1))
    total = ((below + above) + (behind + ahead)) + (left + right)
    return kappa * (total - 6.0 * mid) - advect * (mid - behind)


def put_ring(ref, z, value):
    nx = value.shape[0]
    ref[z, pl.ds(8, nx)] = value
    ref[z, 7:8] = value[nx - 1 : nx]
    ref[z, 8 + nx : 9 + nx] = value[0:1]


def pair_mean(block):
    nx = block.shape[0]
    return (block[pl.ds(0, nx // 2, stride=2), :] + block[pl.ds(1, nx // 2, stride=2), :]) * 0.125


def whole(shape):
    return pl.BlockSpec(shape, lambda i, *_: (0,) * len(shape))


def node_block(j, nz, nx, ny):
    return pl.BlockSpec((1, 1, nz, nx, ny), lambda i, *_: (0, j, 0, 0, 0))


SMEM = pl.BlockSpec(memory_space=pltpu.SMEM)
VMEM = pl.BlockSpec(memory_space=pltpu.VMEM)
ANY = pl.BlockSpec(memory_space=pl.ANY)


def weigh_kernel(info, table, nodes, labels, weighted, kappa, block):
    first = (info[0] == 0).astype(F32)
    total = None
    for z in range(nodes.shape[2]):
        value = float(WEIGHTS[1]) * nodes[0, 1, z]
        for j in range(2, NODES):
            value = value + float(WEIGHTS[j]) * nodes[0, j, z]
        weighted[z] = value + (first * float(WEIGHTS[0])) * nodes[0, 0, z]
        cells = kappa_of(labels[z], table)
        total = cells if z == 0 else total + cells
    block[...] = total
    kappa[0] = pair_mean(block)


def weigh(info, table, node_fields, labels):
    _, _, nz, nx, ny = node_fields.shape
    cut = 4
    return pl.pallas_call(
        weigh_kernel,
        grid=(nz // cut,),
        in_specs=[
            SMEM, SMEM,
            pl.BlockSpec((1, NODES, cut, nx, ny), lambda i: (0, 0, i, 0, 0)),
            pl.BlockSpec((cut, nx, ny), lambda i: (i, 0, 0)),
        ],
        out_specs=[
            pl.BlockSpec((cut, nx, ny), lambda i: (i, 0, 0)),
            pl.BlockSpec((1, nx // 2, ny), lambda i: (i, 0, 0)),
        ],
        out_shape=[
            jax.ShapeDtypeStruct((nz, nx, ny), F32),
            jax.ShapeDtypeStruct((nz // 4, nx // 2, ny), F32),
        ],
        scratch_shapes=[pltpu.VMEM((nx, ny), F32)],
        compiler_params=pltpu.CompilerParams(vmem_limit_bytes=16 * MIB),
        name="weigh",
    )(info, table, node_fields, labels)


def residual_kernel(
    info, table, weighted, arrived, u0, u4, labels, label_low, label_high, shift,
    coarse, start, wide, block,
):
    nz, nx, ny = weighted.shape
    first = info[0] == 0
    advect = shift[...].astype(F32)
    w0 = float(WEIGHTS[0])
    blank = jnp.zeros((nx, ny), F32)
    wide[0, pl.ds(8, nx)] = blank
    wide[nz + 1, pl.ds(8, nx)] = blank
    for z in range(nz):
        put_ring(wide, z + 1, weighted[z] + w0 * arrived[z])
    for zb in range(nz // 4):
        total = None
        for k in range(4):
            z = 4 * zb + k
            begin = jnp.where(first, u0[0, 0, z], arrived[z])
            start[z] = begin
            value = begin - u4[0, 0, z] + rate(
                wide[z, pl.ds(8, nx)], wide[z + 1, pl.ds(8, nx)], wide[z + 2, pl.ds(8, nx)],
                wide[z + 1, pl.ds(7, nx)], wide[z + 1, pl.ds(9, nx)],
                kappa_of(labels[z], table), advect,
            )
            total = value if total is None else total + value
        block[...] = total
        coarse[zb] = pair_mean(block)
    block[...] = kappa_of(label_low[nz - 1], table) * wide[1, pl.ds(8, nx)]
    coarse[nz // 4] = pair_mean(block)
    block[...] = kappa_of(label_high[0], table) * wide[nz, pl.ds(8, nx)]
    coarse[nz // 4 + 1] = pair_mean(block)


def residual(info, table, weighted, arrived, node_fields, labels, label_low, label_high, shift):
    nz, nx, ny = weighted.shape
    slab = whole((nz, nx, ny))
    return pl.pallas_call(
        residual_kernel,
        grid=(1,),
        in_specs=[
            SMEM, SMEM, slab, slab, node_block(0, nz, nx, ny), node_block(NODES - 1, nz, nx, ny),
            slab, slab, slab, whole((1, ny)),
        ],
        out_specs=[whole((nz // 4 + 2, nx // 2, ny)), slab],
        out_shape=[
            jax.ShapeDtypeStruct((nz // 4 + 2, nx // 2, ny), F32),
            jax.ShapeDtypeStruct((nz, nx, ny), F32),
        ],
        scratch_shapes=[pltpu.VMEM((nz + 2, nx + 16, ny), F32), pltpu.VMEM((nx, ny), F32)],
        compiler_params=pltpu.CompilerParams(vmem_limit_bytes=20 * MIB),
        name="residual",
    )(info, table, weighted, arrived, node_fields, node_fields, labels, label_low, label_high, shift)


def pack_kernel(nodes, start, packed):
    for z in range(nodes.shape[2]):
        u = [start[z]] + [nodes[0, j, z] for j in range(1, NODES)]
        for m in range(STEPS):
            coef = [float(Q[m, j]) for j in range(NODES)]
            if m > 0:
                coef[m] -= float(DT[m])
            total = coef[0] * u[0]
            for j in range(1, NODES):
                total = total + coef[j] * u[j]
            packed[m, z] = total
        packed[STEPS, z] = u[0]


def pack(node_fields, start):
    _, _, nz, nx, ny = node_fields.shape
    cut = 2
    return pl.pallas_call(
        pack_kernel,
        grid=(nz // cut,),
        in_specs=[
            pl.BlockSpec((1, NODES, cut, nx, ny), lambda i: (0, 0, i, 0, 0)),
            pl.BlockSpec((cut, nx, ny), lambda i: (i, 0, 0)),
        ],
        out_specs=pl.BlockSpec((NODES, cut, nx, ny), lambda i: (0, i, 0, 0)),
        out_shape=jax.ShapeDtypeStruct((NODES, nz, nx, ny), F32),
        compiler_params=pltpu.CompilerParams(vmem_limit_bytes=16 * MIB),
        name="pack",
    )(node_fields, start)


def coarse_step(src, dst, kappa, half):
    nz, nx, ny = kappa.shape
    lane = lax.broadcasted_iota(jnp.int32, (8, ny), 1)
    for x in range(0, nx, 8):
        rows = pl.ds(8 + x, 8)
        below, mid = src[0, rows], src[1, rows]
        for z in range(nz):
            above = src[z + 2, rows]
            past = src[z + 1, pl.ds(7 + x, 8)]
            ahead = src[z + 1, pl.ds(9 + x, 8)]
            left = jnp.where(lane == 0, 0.0, pltpu.roll(mid, 1, 1))
            right = jnp.where(lane == ny - 1, 0.0, pltpu.roll(mid, ny - 1, 1))
            total = (below + above) * 0.0625 + (past + ahead) * 0.25 + ((left + right) - 2.625 * mid)
            value = mid + kappa[z, pl.ds(x, 8)] * total - half * (mid - past)
            dst[z + 1, rows] = value
            if x == 0:
                dst[z + 1, 8 + nx : 9 + nx] = value[0:1]
            if x == nx - 8:
                dst[z + 1, 7:8] = value[7:8]
            below, mid = mid, above


def clear_edges(*buffers):
    for ref in buffers:
        nz, nx = ref.shape[0] - 2, ref.shape[1] - 16
        blank = jnp.zeros((nx, ref.shape[2]), F32)
        ref[0, pl.ds(8, nx)] = blank
        ref[nz + 1, pl.ds(8, nx)] = blank


def get_layer(state, z):
    return state[z + 1, pl.ds(8, state.shape[1] - 16)]


def add_layers(state, member, nz):
    for z in range(nz):
        put_ring(state, z + 1, get_layer(state, z) + member[z])


def entry_kernel(info, gathered, shift, field, packet):
    ns, parts, nx, ny = gathered.shape
    for s in range(ns):
        low = gathered[s, 0]
        high = gathered[s, 1]
        if s > 0:
            low = low + gathered[s - 1, 3]
        if s < ns - 1:
            high = high + gathered[s + 1, 2]
        field[2 * s] = low
        field[2 * s + 1] = high
    core = info[4] % 2
    for k in range(ns):
        packet[pl.ds(k * nx, nx)] = field[core * ns + k]
    packet[pl.ds(ns * nx, 8)] = jnp.broadcast_to(shift[...].astype(F32) * 0.5, (8, ny))


def chain_entry(info, gathered, shift):
    ns, _, nx, ny = gathered.shape
    return pl.pallas_call(
        entry_kernel,
        in_specs=[SMEM, VMEM, VMEM],
        out_specs=[VMEM] * 2,
        out_shape=[
            jax.ShapeDtypeStruct((2 * ns, nx, ny), F32),
            jax.ShapeDtypeStruct((ns * nx + 8, ny), F32),
        ],
        compiler_params=pltpu.CompilerParams(vmem_limit_bytes=8 * MIB),
        name="chain_entry",
    )(info, gathered, shift)


def place(members, slot, core, mine, theirs):
    _, nz, nx, _ = members.shape
    half = nz // 2
    for k in range(half):
        members[slot, core * half + k] = mine[pl.ds(k * nx, nx)]
        members[slot, (1 - core) * half + k] = theirs[pl.ds(k * nx, nx)]


def halves_of(halves, base, ref, row, count):
    for j in range(count):
        halves[base + j] = jnp.broadcast_to(ref[row + j : row + j + 1], halves.shape[1:])


def level_kernel(length, axis, info, own, tail, before, kappa, *refs):
    packets, (packet, full, after, members, halves, ping, pong, saved) = refs[:6], refs[6:]
    nz, nx, ny = kappa.shape
    core, position = info[4] % 2, info[axis]
    inner = info[3] if length > 1 else 0
    base = nz // 2 * nx
    for z in range(nz):
        members[position, z] = own[z]
    halves_of(halves, position * length, tail, base, length)
    for k in range(1, 4):
        slot = (position + (4 - k)) % 4
        mine, theirs = packets[2 * (k - 1)], packets[2 * (k - 1) + 1]
        place(members, slot, core, mine, theirs)
        halves_of(halves, slot * length, mine, base, length)
    clear_edges(ping, pong)
    for z in range(nz):
        put_ring(ping, z + 1, members[0, z])
    saved[...] = jnp.zeros(saved.shape, F32)

    def member(group, here, there):
        for j in range(length):
            @pl.when((group == position) & (j == inner))
            def _(here=here):
                for z in range(nz):
                    saved[z] = get_layer(here, z)

            coarse_step(here, there, kappa, halves[group * length + j])
            here, there = there, here
        add_layers(here, members.at[group], nz)
        return here

    if length % 2:
        last, other = ping, pong
        for group in range(1, 4):
            last, other = member(group, last, other), last
    else:
        lax.fori_loop(1, 4, lambda group, _: (member(group, ping, pong), 0)[1], 0)
        last = ping
    after[...] = saved[...] + before[...] if length > 1 else saved[...]
    for z in range(nz):
        full[z] = get_layer(last, z)
    for k in range(nz // 2):
        packet[pl.ds(k * nx, nx)] = full[core * (nz // 2) + k]
    for j in range(4 * length):
        packet[base + j : base + j + 1] = halves[j, 0:1]
    if length == 1:
        packet[base + 4 : base + 8] = halves[0, 0:4]


def chain_level(length, axis, info, own, tail, before, kappa, packets):
    nz, nx, ny = kappa.shape
    return pl.pallas_call(
        functools.partial(level_kernel, length, axis),
        in_specs=[SMEM] + [VMEM] * (4 + len(packets)),
        out_specs=[VMEM] * 3,
        out_shape=[
            jax.ShapeDtypeStruct((nz // 2 * nx + max(8, 4 * length), ny), F32),
            jax.ShapeDtypeStruct((nz, nx, ny), F32),
            jax.ShapeDtypeStruct((nz, nx, ny), F32),
        ],
        scratch_shapes=[
            pltpu.VMEM((4, nz, nx, ny), F32),
            pltpu.VMEM((4 * length, 8, ny), F32),
            pltpu.VMEM((nz + 2, nx + 16, ny), F32),
            pltpu.VMEM((nz + 2, nx + 16, ny), F32),
            pltpu.VMEM((nz, nx, ny), F32),
        ],
        compiler_params=pltpu.CompilerParams(vmem_limit_bytes=12 * MIB),
        name=f"chain_level_{length}",
    )(info, own, tail, before, kappa, *packets)


def final_kernel(info, field, tail, before, kappa, *refs):
    packets, (coarse, members, halves, ping, pong) = refs[:6], refs[6:]
    nz, nx, ny = kappa.shape
    core, zh = info[4] % 2, info[1]
    inside = info[2] * 4 + info[3]
    base = nz // 2 * nx
    halves_of(halves, zh * 16, tail, base, 16)
    for k in range(1, 4):
        slot = (zh + (4 - k)) % 4
        mine, theirs = packets[2 * (k - 1)], packets[2 * (k - 1) + 1]
        place(members, slot, core, mine, theirs)
        halves_of(halves, slot * 16, mine, base, 16)
    begin = zh * 16
    clear_edges(ping, pong)
    for z in range(nz):
        put_ring(ping, z + 1, jnp.where(zh > 0, members[0, z], 0.0))

    def pair(t, _):
        coarse_step(ping, pong, kappa, halves[2 * t])
        coarse_step(pong, ping, kappa, halves[2 * t + 1])
        return 0

    def group(g, _):
        lax.fori_loop(8 * g, 8 * g + 8, pair, 0)
        add_layers(ping, members.at[g], nz)
        return 0

    lax.fori_loop(1, zh, group, 0)

    @pl.when(zh > 0)
    def _():
        lax.fori_loop(8 * zh, 8 * zh + inside // 2, pair, 0)

        @pl.when(inside % 2 == 1)
        def _():
            coarse_step(ping, pong, kappa, halves[begin + inside - 1])
            for z in range(nz):
                put_ring(ping, z + 1, get_layer(pong, z))

    add_layers(ping, before, nz)
    coarse_step(ping, pong, kappa, halves[begin + inside])
    blank = jnp.zeros((nx, ny), F32)
    for f in range(2):
        for edge in range(2):
            coarse[f, edge] = blank
            coarse[f, nz + 2 + edge] = blank
    for z in range(nz):
        value = get_layer(ping, z)
        coarse[0, z + 2] = value
        coarse[1, z + 2] = get_layer(pong, z) + field[z] - value


def chain_final(info, field, tail, before, kappa, packets):
    nz, nx, ny = kappa.shape
    return pl.pallas_call(
        final_kernel,
        in_specs=[SMEM] + [VMEM] * (4 + len(packets)),
        out_specs=VMEM,
        out_shape=jax.ShapeDtypeStruct((2, nz + 4, nx, ny), F32),
        scratch_shapes=[
            pltpu.VMEM((4, nz, nx, ny), F32),
            pltpu.VMEM((64, 8, ny), F32),
            pltpu.VMEM((nz + 2, nx + 16, ny), F32),
            pltpu.VMEM((nz + 2, nx + 16, ny), F32),
        ],
        compiler_params=pltpu.CompilerParams(vmem_limit_bytes=12 * MIB),
        name="chain_final",
    )(info, field, tail, before, kappa, *packets)


CHUNK = 32


def sweeps_kernel(
    info, table, coarse, own, low, high, labels, labels_low, labels_high, shift, out,
    held, marks, lift, kappa, first, mixed_a, mixed_b, *rest,
):
    fields, second, (sems, out_sems) = rest[:STEPS], rest[STEPS : 2 * STEPS], rest[2 * STEPS :]
    mixed = (mixed_a, mixed_b)
    nz, nx, ny = labels.shape
    wide = 3 * nz
    space = info[4]
    copies = []
    for k, (src, mark) in enumerate(((low, labels_low), (own, labels), (high, labels_high))):
        copies.append(
            pltpu.make_async_copy(mark, marks.at[pl.ds(k * nz, nz)], sems.at[2 * k])
        )
        copies.append(
            pltpu.make_async_copy(src, held.at[:, pl.ds(k * nz, nz)], sems.at[2 * k + 1])
        )
    for copy in copies:
        copy.start()
    advect = jnp.broadcast_to(shift[...].astype(F32), (CHUNK, ny))
    for f in range(2):
        for k in range(wide // 4):
            value = coarse[f, space * (nz // 4) + k]
            lift[f, k, pl.ds(0, nx // 2, stride=2), :] = value
            lift[f, k, pl.ds(1, nx // 2, stride=2), :] = value
    for copy in copies:
        copy.wait()

    def layers(low, high, body):
        lax.fori_loop(low, high, lambda z, _: (body(z), 0)[1], 0, unroll=True)

    def mix(slot, z, c, value):
        ref = mixed[slot]
        ref[z, pl.ds(8 + c, CHUNK)] = value
        if c == 0:
            ref[z, 8 + nx : 9 + nx] = value[0:1]
        if c == nx - CHUNK:
            ref[z, 7:8] = value[CHUNK - 1 : CHUNK]

    def opening(z):
        inside = ((z >= nz) | (space > 0)) & ((z < 2 * nz) | (space < 3))
        at = z // 4
        for c in range(0, nx, CHUNK):
            rows = pl.ds(c, CHUNK)
            kappa[z, rows] = jnp.where(inside, kappa_of(marks[z, rows], table), 0.0)
            begin, grow = lift[0, at, rows], lift[1, at, rows]
            first[z, rows] = held[STEPS, z, rows] + begin
            value = held[0, z, rows] + float(DT[0]) * begin + float(0.5 * DT[0] ** 2) * grow
            mix(0, z, c, value)

    layers(0, wide, opening)

    def later_sum(m, z, rows, newest):
        total = None
        for j in range(NODES):
            coef = float(Q[m, j] - (DT[m] if m == j else 0.0))
            node = first[z, rows] if j == 0 else fields[j - 1][z, rows]
            if j == NODES - 1 and newest is not None:
                node = newest
            total = coef * node if total is None else total + coef * node
        return total

    outs = [pltpu.make_async_copy(first.at[pl.ds(nz, nz)], out.at[0, 0], out_sems.at[0])]
    outs[0].start()
    for turn in range(2 * STEPS):
        sweep, m = turn // STEPS, turn % STEPS
        past = first if m == 0 else (fields if sweep == 0 else second)[m - 1]
        target = (fields if sweep == 0 else second)[m]
        now, later = turn % 2, (turn + 1) % 2

        def stage(z, turn=turn, sweep=sweep, m=m, past=past, target=target, now=now, later=later):
            source = mixed[now]
            for c in range(0, nx, CHUNK):
                rows, inner = pl.ds(c, CHUNK), pl.ds(8 + c, CHUNK)
                value = past[z, rows] + rate(
                    source[z - 1, inner], source[z, inner], source[z + 1, inner],
                    source[z, pl.ds(7 + c, CHUNK)], source[z, pl.ds(9 + c, CHUNK)],
                    kappa[z, rows], advect,
                )
                target[z, rows] = value
                if turn == 2 * STEPS - 1:
                    continue
                if turn < STEPS - 1:
                    blend = (
                        float(DT[m + 1]) * value
                        + held[m + 1, z, rows]
                        + float(0.5 * DT[m + 1] ** 2) * lift[1, z // 4, rows]
                    )
                elif turn == STEPS - 1:
                    blend = later_sum(0, z, rows, value) + float(DT[0]) * first[z, rows]
                else:
                    blend = later_sum(m + 1, z, rows, None) + float(DT[m + 1]) * value
                mix(later, z, c, blend)

        layers(turn + 1, wide - 1 - turn, stage)
        if sweep == 1:
            copy = pltpu.make_async_copy(
                target.at[pl.ds(nz, nz)], out.at[0, m + 1], out_sems.at[m + 1]
            )
            copy.start()
            outs.append(copy)
    for copy in outs:
        copy.wait()


def fine_sweeps(info, table, coarse, own, low, high, labels, labels_low, labels_high, shift):
    nz, nx, ny = labels.shape
    wide = 3 * nz
    return pl.pallas_call(
        sweeps_kernel,
        in_specs=[SMEM, SMEM, VMEM] + [ANY] * 6 + [VMEM],
        out_specs=ANY,
        out_shape=jax.ShapeDtypeStruct((1, NODES, nz, nx, ny), F32),
        scratch_shapes=[
            pltpu.VMEM((NODES, wide, nx, ny), F32),
            pltpu.VMEM((wide, nx, ny), jnp.int32),
            pltpu.VMEM((2, wide // 4, nx, ny), F32),
            pltpu.VMEM((wide, nx, ny), F32),
            pltpu.VMEM((wide, nx, ny), F32),
            pltpu.VMEM((wide, nx + 16, ny), F32),
            pltpu.VMEM((wide, nx + 16, ny), F32),
        ]
        + [pltpu.VMEM((wide, nx, ny), F32)] * (2 * STEPS)
        + [
            pltpu.SemaphoreType.DMA((6,)),
            pltpu.SemaphoreType.DMA((NODES,)),
        ],
        compiler_params=pltpu.CompilerParams(vmem_limit_bytes=36 * MIB),
        name="fine_sweeps",
    )(info, table, coarse, own, low, high, labels, labels_low, labels_high, shift)


def to_space(value, by):
    return lax.ppermute(value, "space", [(i, i + by) for i in range(4) if 0 <= i + by < 4])


def to_next(value, by):
    axes = TM + ("space",)
    pairs = [
        (4 * n + s, 4 * (n + 1) + s + by) for n in range(63) for s in range(4) if 0 <= s + by < 4
    ]
    return lax.ppermute(value, axes, pairs)


def swap_core(value):
    return lax.ppermute(value, "space", [(0, 1), (1, 0), (2, 3), (3, 2)])


def gather_axis(packet, axis):
    packets = []
    for k in range(1, 4):
        got = lax.ppermute(packet, axis, [(i, (i + k) % 4) for i in range(4)])
        packets += [got, swap_core(got)]
    return packets


def shards(node_fields, region_label, sheet_shift, diffusivity):
    zh, y, x = (lax.axis_index(a) for a in TM)
    space = lax.axis_index("space")
    info = jnp.stack([zh * 16 + y * 4 + x, zh, y, x, space]).astype(jnp.int32)
    arrived = to_next(node_fields[0, NODES - 1], 0)
    labels_low, labels_high = to_space(region_label, 1), to_space(region_label, -1)
    weighted, kappa = weigh(info, diffusivity, node_fields, region_label)
    kappa = lax.all_gather(kappa, "space", axis=0, tiled=True)
    weighted, kappa = lax.optimization_barrier((weighted, kappa))
    coarse, start = residual(
        info, diffusivity, weighted, arrived, node_fields, region_label, labels_low, labels_high,
        sheet_shift,
    )
    gathered = lax.all_gather(coarse, "space", axis=0, tiled=False)
    field, packet = chain_entry(info, gathered, sheet_shift)
    packets = gather_axis(packet, "x")
    start, _ = lax.optimization_barrier((start, packet))
    packed = pack(node_fields, start)
    packed, packets[4] = lax.optimization_barrier((packed, packets[4]))
    packed_low, packed_high = to_space(packed, 1), to_space(packed, -1)
    packet, field4, prefix = chain_level(1, 3, info, field, packet, field, kappa, packets)
    packets = gather_axis(packet, "y")
    packet, _, prefix = chain_level(4, 2, info, field4, packet, prefix, kappa, packets)
    packets = gather_axis(packet, "zh")
    correction = chain_final(info, field, packet, prefix, kappa, packets)
    return fine_sweeps(
        info, diffusivity, correction, packed, packed_low, packed_high,
        region_label, labels_low, labels_high, sheet_shift,
    )


def solution(mesh):
    grid = Mesh(mesh.devices.reshape(4, 4, 4, 4), TM + ("space",))
    in_specs = (P(TM, None, "space", None, None), P("space", None, None), P(TM, None), P())
    out_specs = P(TM, None, "space", None, None)
    return jax.shard_map(shards, mesh=grid, in_specs=in_specs, out_specs=out_specs, check_vma=False)
```

```python
import functools
import math

import jax
import jax.numpy as jnp
import numpy as np
from jax import lax
from jax.experimental import pallas as pl
from jax.experimental.pallas import tpu as pltpu
from jax.sharding import Mesh
from jax.sharding import PartitionSpec as P

NODES = 5
STEPS = NODES - 1
F32 = jnp.float32
TM = ("zh", "y", "x")
MIB = 1 << 20


def node_tables():
    radius = math.sqrt(3.0 / 7.0)
    points = [0.0, (1.0 - radius) / 2.0, 0.5, (1.0 + radius) / 2.0, 1.0]
    integrals = np.zeros((4, 5))
    for column in range(5):
        coeffs = [1.0]
        divisor = 1.0
        for other in range(5):
            if other != column:
                anchor = points[other]
                product = [0.0] * (len(coeffs) + 1)
                for degree in range(len(coeffs)):
                    product[degree + 1] = product[degree + 1] + coeffs[degree]
                    product[degree] = product[degree] - anchor * coeffs[degree]
                coeffs = product
                divisor = divisor * (points[column] - anchor)
        for row in range(4):
            bottom = points[row]
            summit = points[row + 1]
            amount = 0.0
            for degree in range(len(coeffs)):
                amount = amount + coeffs[degree] / (degree + 1) * (
                    summit ** (degree + 1) - bottom ** (degree + 1)
                )
            integrals[row, column] = amount / divisor
    return (np.array(points), integrals)


TAU, Q = node_tables()
WEIGHTS = Q.sum(axis=0)
DT = TAU[1:] - TAU[:-1]


def kappa_of(labels, table):
    value = jnp.where(labels == 3, table[3], 0.0)
    for region in range(3):
        value = jnp.where(labels == region, table[region], value)
    return value


def rate(below, mid, above, behind, ahead, kappa, advect):
    cols = mid.shape[1]
    lane = lax.broadcasted_iota(jnp.int32, mid.shape, 1)
    left = jnp.where(lane == 0, 0.0, pltpu.roll(mid, 1, 1))
    right = jnp.where(lane == cols - 1, 0.0, pltpu.roll(mid, cols - 1, 1))
    total = ((below + above) + (behind + ahead)) + (left + right)
    return kappa * (total - 6.0 * mid) - advect * (mid - behind)


def put_ring(ref, z, value):
    nx = value.shape[0]
    ref[z, pl.ds(8, nx)] = value
    ref[z, 7:8] = value[nx - 1 : nx]
    ref[z, 8 + nx : 9 + nx] = value[0:1]


def pair_mean(block):
    nx = block.shape[0]
    return (block[pl.ds(0, nx // 2, stride=2), :] + block[pl.ds(1, nx // 2, stride=2), :]) * 0.125


def whole(shape):
    return pl.BlockSpec(shape, lambda i, *_: (0,) * len(shape))


def node_block(j, nz, nx, ny):
    return pl.BlockSpec((1, 1, nz, nx, ny), lambda i, *_: (0, j, 0, 0, 0))


SMEM = pl.BlockSpec(memory_space=pltpu.SMEM)
VMEM = pl.BlockSpec(memory_space=pltpu.VMEM)
ANY = pl.BlockSpec(memory_space=pl.ANY)


def weigh_kernel(info, table, nodes, labels, weighted, kappa, block):
    first = (info[0] == 0).astype(F32)
    total = None
    for z in range(nodes.shape[2]):
        value = float(WEIGHTS[1]) * nodes[0, 1, z]
        for j in range(2, NODES):
            value = value + float(WEIGHTS[j]) * nodes[0, j, z]
        weighted[z] = value + (first * float(WEIGHTS[0])) * nodes[0, 0, z]
        cells = kappa_of(labels[z], table)
        total = cells if z == 0 else total + cells
    block[...] = total
    kappa[0] = pair_mean(block)


def weigh(info, table, node_fields, labels):
    _, _, nz, nx, ny = node_fields.shape
    cut = 4
    return pl.pallas_call(
        weigh_kernel,
        grid=(nz // cut,),
        in_specs=[
            SMEM, SMEM,
            pl.BlockSpec((1, NODES, cut, nx, ny), lambda i: (0, 0, i, 0, 0)),
            pl.BlockSpec((cut, nx, ny), lambda i: (i, 0, 0)),
        ],
        out_specs=[
            pl.BlockSpec((cut, nx, ny), lambda i: (i, 0, 0)),
            pl.BlockSpec((1, nx // 2, ny), lambda i: (i, 0, 0)),
        ],
        out_shape=[
            jax.ShapeDtypeStruct((nz, nx, ny), F32),
            jax.ShapeDtypeStruct((nz // 4, nx // 2, ny), F32),
        ],
        scratch_shapes=[pltpu.VMEM((nx, ny), F32)],
        compiler_params=pltpu.CompilerParams(vmem_limit_bytes=16 * MIB),
        name="weigh",
    )(info, table, node_fields, labels)


def residual_kernel(
    info, table, weighted, arrived, u0, u4, labels, label_low, label_high, shift, cells,
    coarse, start, wide, block,
):
    nz, nx, ny = weighted.shape
    first = info[0] == 0
    advect = shift[...].astype(F32)
    w0 = float(WEIGHTS[0])
    blank = jnp.zeros((nx, ny), F32)
    wide[0, pl.ds(8, nx)] = blank
    wide[nz + 1, pl.ds(8, nx)] = blank
    for z in range(nz):
        put_ring(wide, z + 1, weighted[z] + w0 * arrived[z])
    for zb in range(nz // 4):
        total = None
        for k in range(4):
            z = 4 * zb + k
            begin = jnp.where(first, u0[0, 0, z], arrived[z])
            start[z] = begin
            value = begin - u4[0, 0, z] + rate(
                wide[z, pl.ds(8, nx)], wide[z + 1, pl.ds(8, nx)], wide[z + 2, pl.ds(8, nx)],
                wide[z + 1, pl.ds(7, nx)], wide[z + 1, pl.ds(9, nx)],
                kappa_of(labels[z], table), advect,
            )
            total = value if total is None else total + value
        block[...] = total
        coarse[zb] = pair_mean(block)
    block[...] = kappa_of(label_low[nz - 1], table) * wide[1, pl.ds(8, nx)]
    coarse[nz // 4] = pair_mean(block)
    block[...] = kappa_of(label_high[0], table) * wide[nz, pl.ds(8, nx)]
    coarse[nz // 4 + 1] = pair_mean(block)
    coarse[nz // 4 + 2] = cells[0]
    coarse[nz // 4 + 3] = cells[1]


def residual(
    info, table, weighted, arrived, node_fields, labels, label_low, label_high, shift, cells
):
    nz, nx, ny = weighted.shape
    slab = whole((nz, nx, ny))
    return pl.pallas_call(
        residual_kernel,
        grid=(1,),
        in_specs=[
            SMEM, SMEM, slab, slab, node_block(0, nz, nx, ny), node_block(NODES - 1, nz, nx, ny),
            slab, slab, slab, whole((1, ny)), whole(cells.shape),
        ],
        out_specs=[whole((nz // 4 + 4, nx // 2, ny)), slab],
        out_shape=[
            jax.ShapeDtypeStruct((nz // 4 + 4, nx // 2, ny), F32),
            jax.ShapeDtypeStruct((nz, nx, ny), F32),
        ],
        scratch_shapes=[pltpu.VMEM((nz + 2, nx + 16, ny), F32), pltpu.VMEM((nx, ny), F32)],
        compiler_params=pltpu.CompilerParams(vmem_limit_bytes=20 * MIB),
        name="residual",
    )(
        info, table, weighted, arrived, node_fields, node_fields, labels, label_low, label_high,
        shift, cells,
    )


def pack_kernel(nodes, start, packed):
    for z in range(nodes.shape[2]):
        u = [start[z]] + [nodes[0, j, z] for j in range(1, NODES)]
        for m in range(STEPS):
            coef = [float(Q[m, j]) for j in range(NODES)]
            if m > 0:
                coef[m] -= float(DT[m])
            total = coef[0] * u[0]
            for j in range(1, NODES):
                total = total + coef[j] * u[j]
            packed[m, z] = total
        packed[STEPS, z] = u[0]


def pack(node_fields, start):
    _, _, nz, nx, ny = node_fields.shape
    cut = 2
    return pl.pallas_call(
        pack_kernel,
        grid=(nz // cut,),
        in_specs=[
            pl.BlockSpec((1, NODES, cut, nx, ny), lambda i: (0, 0, i, 0, 0)),
            pl.BlockSpec((cut, nx, ny), lambda i: (i, 0, 0)),
        ],
        out_specs=pl.BlockSpec((NODES, cut, nx, ny), lambda i: (0, i, 0, 0)),
        out_shape=jax.ShapeDtypeStruct((NODES, nz, nx, ny), F32),
        compiler_params=pltpu.CompilerParams(vmem_limit_bytes=16 * MIB),
        name="pack",
    )(node_fields, start)


def coarse_step(src, dst, kappa, half):
    nz, nx, ny = kappa.shape
    lane = lax.broadcasted_iota(jnp.int32, (8, ny), 1)
    for x in range(0, nx, 8):
        rows = pl.ds(8 + x, 8)
        below, mid = src[0, rows], src[1, rows]
        for z in range(nz):
            above = src[z + 2, rows]
            past = src[z + 1, pl.ds(7 + x, 8)]
            ahead = src[z + 1, pl.ds(9 + x, 8)]
            left = jnp.where(lane == 0, 0.0, pltpu.roll(mid, 1, 1))
            right = jnp.where(lane == ny - 1, 0.0, pltpu.roll(mid, ny - 1, 1))
            total = (below + above) * 0.0625 + (past + ahead) * 0.25 + ((left + right) - 2.625 * mid)
            value = mid + kappa[z, pl.ds(x, 8)] * total - half * (mid - past)
            dst[z + 1, rows] = value
            if x == 0:
                dst[z + 1, 8 + nx : 9 + nx] = value[0:1]
            if x == nx - 8:
                dst[z + 1, 7:8] = value[7:8]
            below, mid = mid, above


def clear_edges(*buffers):
    for ref in buffers:
        nz, nx = ref.shape[0] - 2, ref.shape[1] - 16
        blank = jnp.zeros((nx, ref.shape[2]), F32)
        ref[0, pl.ds(8, nx)] = blank
        ref[nz + 1, pl.ds(8, nx)] = blank


def get_layer(state, z):
    return state[z + 1, pl.ds(8, state.shape[1] - 16)]


def add_layers(state, member, nz):
    for z in range(nz):
        put_ring(state, z + 1, get_layer(state, z) + member[z])


def entry_kernel(info, gathered, shift, field, kappa, packet):
    ns, parts, nx, ny = gathered.shape
    for s in range(ns):
        low = gathered[s, 0]
        high = gathered[s, 1]
        if s > 0:
            low = low + gathered[s - 1, 3]
        if s < ns - 1:
            high = high + gathered[s + 1, 2]
        field[2 * s] = low
        field[2 * s + 1] = high
        kappa[2 * s] = gathered[s, 4]
        kappa[2 * s + 1] = gathered[s, 5]
    core = info[4] % 2
    for k in range(ns):
        packet[pl.ds(k * nx, nx)] = field[core * ns + k]
    packet[pl.ds(ns * nx, 8)] = jnp.broadcast_to(shift[...].astype(F32) * 0.5, (8, ny))


def chain_entry(info, gathered, shift):
    ns, _, nx, ny = gathered.shape
    return pl.pallas_call(
        entry_kernel,
        in_specs=[SMEM, VMEM, VMEM],
        out_specs=[VMEM] * 3,
        out_shape=[
            jax.ShapeDtypeStruct((2 * ns, nx, ny), F32),
            jax.ShapeDtypeStruct((2 * ns, nx, ny), F32),
            jax.ShapeDtypeStruct((ns * nx + 8, ny), F32),
        ],
        compiler_params=pltpu.CompilerParams(vmem_limit_bytes=8 * MIB),
        name="chain_entry",
    )(info, gathered, shift)


def place(members, slot, core, mine, theirs):
    _, nz, nx, _ = members.shape
    half = nz // 2
    for k in range(half):
        members[slot, core * half + k] = mine[pl.ds(k * nx, nx)]
        members[slot, (1 - core) * half + k] = theirs[pl.ds(k * nx, nx)]


def halves_of(halves, base, ref, row, count):
    for j in range(count):
        halves[base + j] = jnp.broadcast_to(ref[row + j : row + j + 1], halves.shape[1:])


def level_kernel(length, axis, info, own, tail, before, kappa, *refs):
    packets, (packet, full, after, members, halves, ping, pong, saved) = refs[:6], refs[6:]
    nz, nx, ny = kappa.shape
    core, position = info[4] % 2, info[axis]
    inner = info[3] if length > 1 else 0
    base = nz // 2 * nx
    for z in range(nz):
        members[position, z] = own[z]
    halves_of(halves, position * length, tail, base, length)
    for k in range(1, 4):
        slot = (position + (4 - k)) % 4
        mine, theirs = packets[2 * (k - 1)], packets[2 * (k - 1) + 1]
        place(members, slot, core, mine, theirs)
        halves_of(halves, slot * length, mine, base, length)
    clear_edges(ping, pong)
    for z in range(nz):
        put_ring(ping, z + 1, members[0, z])
    saved[...] = jnp.zeros(saved.shape, F32)

    def member(group, here, there):
        for j in range(length):
            @pl.when((group == position) & (j == inner))
            def _(here=here):
                for z in range(nz):
                    saved[z] = get_layer(here, z)

            coarse_step(here, there, kappa, halves[group * length + j])
            here, there = there, here
        add_layers(here, members.at[group], nz)
        return here

    if length % 2:
        last, other = ping, pong
        for group in range(1, 4):
            last, other = member(group, last, other), last
    else:
        lax.fori_loop(1, 4, lambda group, _: (member(group, ping, pong), 0)[1], 0)
        last = ping
    after[...] = saved[...] + before[...] if length > 1 else saved[...]
    for z in range(nz):
        full[z] = get_layer(last, z)
    for k in range(nz // 2):
        packet[pl.ds(k * nx, nx)] = full[core * (nz // 2) + k]
    for j in range(4 * length):
        packet[base + j : base + j + 1] = halves[j, 0:1]
    if length == 1:
        packet[base + 4 : base + 8] = halves[0, 0:4]


def chain_level(length, axis, info, own, tail, before, kappa, packets):
    nz, nx, ny = kappa.shape
    return pl.pallas_call(
        functools.partial(level_kernel, length, axis),
        in_specs=[SMEM] + [VMEM] * (4 + len(packets)),
        out_specs=[VMEM] * 3,
        out_shape=[
            jax.ShapeDtypeStruct((nz // 2 * nx + max(8, 4 * length), ny), F32),
            jax.ShapeDtypeStruct((nz, nx, ny), F32),
            jax.ShapeDtypeStruct((nz, nx, ny), F32),
        ],
        scratch_shapes=[
            pltpu.VMEM((4, nz, nx, ny), F32),
            pltpu.VMEM((4 * length, 8, ny), F32),
            pltpu.VMEM((nz + 2, nx + 16, ny), F32),
            pltpu.VMEM((nz + 2, nx + 16, ny), F32),
            pltpu.VMEM((nz, nx, ny), F32),
        ],
        compiler_params=pltpu.CompilerParams(vmem_limit_bytes=12 * MIB),
        name=f"chain_level_{length}",
    )(info, own, tail, before, kappa, *packets)


def finish_chain(info, field, tail, before, kappa, packets, coarse, members, halves, ping, pong):
    nz, nx, ny = kappa.shape
    core, zh = info[4] % 2, info[1]
    inside = info[2] * 4 + info[3]
    base = nz // 2 * nx
    halves_of(halves, zh * 16, tail, base, 16)
    for k in range(1, 4):
        slot = (zh + (4 - k)) % 4
        mine, theirs = packets[2 * (k - 1)], packets[2 * (k - 1) + 1]
        place(members, slot, core, mine, theirs)
        halves_of(halves, slot * 16, mine, base, 16)
    begin = zh * 16
    clear_edges(ping, pong)
    for z in range(nz):
        put_ring(ping, z + 1, jnp.where(zh > 0, members[0, z], 0.0))

    def pair(t, _):
        coarse_step(ping, pong, kappa, halves[2 * t])
        coarse_step(pong, ping, kappa, halves[2 * t + 1])
        return 0

    def group(g, _):
        lax.fori_loop(8 * g, 8 * g + 8, pair, 0)
        add_layers(ping, members.at[g], nz)
        return 0

    lax.fori_loop(1, zh, group, 0)

    @pl.when(zh > 0)
    def _():
        lax.fori_loop(8 * zh, 8 * zh + inside // 2, pair, 0)

        @pl.when(inside % 2 == 1)
        def _():
            coarse_step(ping, pong, kappa, halves[begin + inside - 1])
            for z in range(nz):
                put_ring(ping, z + 1, get_layer(pong, z))

    add_layers(ping, before, nz)
    coarse_step(ping, pong, kappa, halves[begin + inside])
    blank = jnp.zeros((nx, ny), F32)
    for f in range(2):
        for edge in range(2):
            coarse[f, edge] = blank
            coarse[f, nz + 2 + edge] = blank
    for z in range(nz):
        value = get_layer(ping, z)
        coarse[0, z + 2] = value
        coarse[1, z + 2] = get_layer(pong, z) + field[z] - value


CHUNK = 32


def sweeps_kernel(
    info, table, own, low, high, labels, labels_low, labels_high, shift,
    field, tail, before, kappa_c, p0, p1, p2, p3, p4, p5, out,
    coarse, members, halves, ping, pong, held, marks, lift, kappa, first, mixed_a, mixed_b, *rest,
):
    fields, second, (sems, out_sems) = rest[:STEPS], rest[STEPS : 2 * STEPS], rest[2 * STEPS :]
    mixed = (mixed_a, mixed_b)
    nz, nx, ny = labels.shape
    wide = 3 * nz
    space = info[4]
    copies = []
    for k, (src, mark) in enumerate(((low, labels_low), (own, labels), (high, labels_high))):
        copies.append(
            pltpu.make_async_copy(mark, marks.at[pl.ds(k * nz, nz)], sems.at[2 * k])
        )
        copies.append(
            pltpu.make_async_copy(src, held.at[:, pl.ds(k * nz, nz)], sems.at[2 * k + 1])
        )
    for copy in copies:
        copy.start()
    finish_chain(
        info, field, tail, before, kappa_c, (p0, p1, p2, p3, p4, p5), coarse, members, halves, ping, pong
    )
    advect = jnp.broadcast_to(shift[...].astype(F32), (CHUNK, ny))
    for f in range(2):
        for k in range(wide // 4):
            value = coarse[f, space * (nz // 4) + k]
            lift[f, k, pl.ds(0, nx // 2, stride=2), :] = value
            lift[f, k, pl.ds(1, nx // 2, stride=2), :] = value
    for copy in copies:
        copy.wait()

    def layers(low, high, body):
        lax.fori_loop(low, high, lambda z, _: (body(z), 0)[1], 0, unroll=True)

    def mix(slot, z, c, value):
        ref = mixed[slot]
        ref[z, pl.ds(8 + c, CHUNK)] = value
        if c == 0:
            ref[z, 8 + nx : 9 + nx] = value[0:1]
        if c == nx - CHUNK:
            ref[z, 7:8] = value[CHUNK - 1 : CHUNK]

    def opening(z):
        inside = ((z >= nz) | (space > 0)) & ((z < 2 * nz) | (space < 3))
        at = z // 4
        for c in range(0, nx, CHUNK):
            rows = pl.ds(c, CHUNK)
            kappa[z, rows] = jnp.where(inside, kappa_of(marks[z, rows], table), 0.0)
            begin, grow = lift[0, at, rows], lift[1, at, rows]
            first[z, rows] = held[STEPS, z, rows] + begin
            value = held[0, z, rows] + float(DT[0]) * begin + float(0.5 * DT[0] ** 2) * grow
            mix(0, z, c, value)

    layers(0, wide, opening)

    def later_sum(m, z, rows, newest):
        total = None
        for j in range(NODES):
            coef = float(Q[m, j] - (DT[m] if m == j else 0.0))
            node = first[z, rows] if j == 0 else fields[j - 1][z, rows]
            if j == NODES - 1 and newest is not None:
                node = newest
            total = coef * node if total is None else total + coef * node
        return total

    outs = [pltpu.make_async_copy(first.at[pl.ds(nz, nz)], out.at[0, 0], out_sems.at[0])]
    outs[0].start()
    for turn in range(2 * STEPS):
        sweep, m = turn // STEPS, turn % STEPS
        past = first if m == 0 else (fields if sweep == 0 else second)[m - 1]
        target = (fields if sweep == 0 else second)[m]
        now, later = turn % 2, (turn + 1) % 2

        def stage(z, turn=turn, sweep=sweep, m=m, past=past, target=target, now=now, later=later):
            source = mixed[now]
            for c in range(0, nx, CHUNK):
                rows, inner = pl.ds(c, CHUNK), pl.ds(8 + c, CHUNK)
                value = past[z, rows] + rate(
                    source[z - 1, inner], source[z, inner], source[z + 1, inner],
                    source[z, pl.ds(7 + c, CHUNK)], source[z, pl.ds(9 + c, CHUNK)],
                    kappa[z, rows], advect,
                )
                target[z, rows] = value
                if turn == 2 * STEPS - 1:
                    continue
                if turn < STEPS - 1:
                    blend = (
                        float(DT[m + 1]) * value
                        + held[m + 1, z, rows]
                        + float(0.5 * DT[m + 1] ** 2) * lift[1, z // 4, rows]
                    )
                elif turn == STEPS - 1:
                    blend = later_sum(0, z, rows, value) + float(DT[0]) * first[z, rows]
                else:
                    blend = later_sum(m + 1, z, rows, None) + float(DT[m + 1]) * value
                mix(later, z, c, blend)

        layers(turn + 1, wide - 1 - turn, stage)
        if sweep == 1:
            copy = pltpu.make_async_copy(
                target.at[pl.ds(nz, nz)], out.at[0, m + 1], out_sems.at[m + 1]
            )
            copy.start()
            outs.append(copy)
    for copy in outs:
        copy.wait()


def fine_sweeps(info, table, fine, chain):
    nz, nx, ny = fine[3].shape
    nzc, nxc, _ = chain[3].shape
    wide = 3 * nz
    return pl.pallas_call(
        sweeps_kernel,
        in_specs=[SMEM, SMEM] + [ANY] * 6 + [VMEM] * 11,
        out_specs=ANY,
        out_shape=jax.ShapeDtypeStruct((1, NODES, nz, nx, ny), F32),
        scratch_shapes=[
            pltpu.VMEM((2, nzc + 4, nxc, ny), F32),
            pltpu.VMEM((4, nzc, nxc, ny), F32),
            pltpu.VMEM((64, 8, ny), F32),
            pltpu.VMEM((nzc + 2, nxc + 16, ny), F32),
            pltpu.VMEM((nzc + 2, nxc + 16, ny), F32),
            pltpu.VMEM((NODES, wide, nx, ny), F32),
            pltpu.VMEM((wide, nx, ny), jnp.int32),
            pltpu.VMEM((2, wide // 4, nx, ny), F32),
            pltpu.VMEM((wide, nx, ny), F32),
            pltpu.VMEM((wide, nx, ny), F32),
            pltpu.VMEM((wide, nx + 16, ny), F32),
            pltpu.VMEM((wide, nx + 16, ny), F32),
        ]
        + [pltpu.VMEM((wide, nx, ny), F32)] * (2 * STEPS)
        + [
            pltpu.SemaphoreType.DMA((6,)),
            pltpu.SemaphoreType.DMA((NODES,)),
        ],
        compiler_params=pltpu.CompilerParams(vmem_limit_bytes=40 * MIB),
        name="fine_sweeps",
    )(info, table, *fine, *chain)


def to_space(value, by):
    return lax.ppermute(value, "space", [(i, i + by) for i in range(4) if 0 <= i + by < 4])


def to_next(value, by):
    axes = TM + ("space",)
    pairs = [
        (4 * n + s, 4 * (n + 1) + s + by) for n in range(63) for s in range(4) if 0 <= s + by < 4
    ]
    return lax.ppermute(value, axes, pairs)


def swap_core(value):
    return lax.ppermute(value, "space", [(0, 1), (1, 0), (2, 3), (3, 2)])


def gather_axis(packet, axis):
    packets = []
    for k in range(1, 4):
        got = lax.ppermute(packet, axis, [(i, (i + k) % 4) for i in range(4)])
        packets += [got, swap_core(got)]
    return packets


def shards(node_fields, region_label, sheet_shift, diffusivity):
    zh, y, x = (lax.axis_index(a) for a in TM)
    space = lax.axis_index("space")
    info = jnp.stack([zh * 16 + y * 4 + x, zh, y, x, space]).astype(jnp.int32)
    arrived = to_next(node_fields[0, NODES - 1], 0)
    labels_low, labels_high = to_space(region_label, 1), to_space(region_label, -1)
    weighted, cells = weigh(info, diffusivity, node_fields, region_label)
    coarse, start = residual(
        info, diffusivity, weighted, arrived, node_fields, region_label, labels_low, labels_high,
        sheet_shift, cells,
    )
    gathered = lax.all_gather(coarse, "space", axis=0, tiled=False)
    field, kappa, packet = chain_entry(info, gathered, sheet_shift)
    packets = gather_axis(packet, "x")
    start, _ = lax.optimization_barrier((start, packet))
    packed = pack(node_fields, start)
    packed, packets[4] = lax.optimization_barrier((packed, packets[4]))
    packed_low, packed_high = to_space(packed, 1), to_space(packed, -1)
    packet, field4, prefix = chain_level(1, 3, info, field, packet, field, kappa, packets)
    packets = gather_axis(packet, "y")
    packet, _, prefix = chain_level(4, 2, info, field4, packet, prefix, kappa, packets)
    packets = gather_axis(packet, "zh")
    return fine_sweeps(
        info,
        diffusivity,
        (packed, packed_low, packed_high, region_label, labels_low, labels_high, sheet_shift),
        (field, packet, prefix, kappa, *packets),
    )


def solution(mesh):
    grid = Mesh(mesh.devices.reshape(4, 4, 4, 4), TM + ("space",))
    in_specs = (P(TM, None, "space", None, None), P("space", None, None), P(TM, None), P())
    out_specs = P(TM, None, "space", None, None)
    return jax.shard_map(shards, mesh=grid, in_specs=in_specs, out_specs=out_specs, check_vma=False)
```

```python
import functools
import math

import jax
import jax.numpy as jnp
import numpy as np
from jax import lax
from jax.experimental import pallas as pl
from jax.experimental.pallas import tpu as pltpu
from jax.sharding import Mesh
from jax.sharding import PartitionSpec as P

NODES = 5
STEPS = NODES - 1
F32 = jnp.float32
TM = ("zh", "y", "x")
MIB = 1 << 20


def node_tables():
    radius = math.sqrt(3.0 / 7.0)
    points = [0.0, (1.0 - radius) / 2.0, 0.5, (1.0 + radius) / 2.0, 1.0]
    integrals = np.zeros((4, 5))
    for column in range(5):
        coeffs = [1.0]
        divisor = 1.0
        for other in range(5):
            if other != column:
                anchor = points[other]
                product = [0.0] * (len(coeffs) + 1)
                for degree in range(len(coeffs)):
                    product[degree + 1] = product[degree + 1] + coeffs[degree]
                    product[degree] = product[degree] - anchor * coeffs[degree]
                coeffs = product
                divisor = divisor * (points[column] - anchor)
        for row in range(4):
            bottom = points[row]
            summit = points[row + 1]
            amount = 0.0
            for degree in range(len(coeffs)):
                amount = amount + coeffs[degree] / (degree + 1) * (
                    summit ** (degree + 1) - bottom ** (degree + 1)
                )
            integrals[row, column] = amount / divisor
    return (np.array(points), integrals)


TAU, Q = node_tables()
WEIGHTS = Q.sum(axis=0)
DT = TAU[1:] - TAU[:-1]


def kappa_of(labels, table):
    value = jnp.where(labels == 3, table[3], 0.0)
    for region in range(3):
        value = jnp.where(labels == region, table[region], value)
    return value


def rate(below, mid, above, behind, ahead, kappa, advect):
    cols = mid.shape[1]
    lane = lax.broadcasted_iota(jnp.int32, mid.shape, 1)
    left = jnp.where(lane == 0, 0.0, pltpu.roll(mid, 1, 1))
    right = jnp.where(lane == cols - 1, 0.0, pltpu.roll(mid, cols - 1, 1))
    total = ((below + above) + (behind + ahead)) + (left + right)
    return kappa * (total - 6.0 * mid) - advect * (mid - behind)


def put_ring(ref, z, value):
    nx = value.shape[0]
    ref[z, pl.ds(8, nx)] = value
    ref[z, 7:8] = value[nx - 1 : nx]
    ref[z, 8 + nx : 9 + nx] = value[0:1]


def pair_mean(block):
    nx = block.shape[0]
    return (block[pl.ds(0, nx // 2, stride=2), :] + block[pl.ds(1, nx // 2, stride=2), :]) * 0.125


def whole(shape):
    return pl.BlockSpec(shape, lambda i, *_: (0,) * len(shape))


def node_block(j, nz, nx, ny):
    return pl.BlockSpec((1, 1, nz, nx, ny), lambda i, *_: (0, j, 0, 0, 0))


SMEM = pl.BlockSpec(memory_space=pltpu.SMEM)
VMEM = pl.BlockSpec(memory_space=pltpu.VMEM)
ANY = pl.BlockSpec(memory_space=pl.ANY)


def weigh_kernel(info, table, nodes, labels, weighted, kappa, block):
    first = (info[0] == 0).astype(F32)
    total = None
    for z in range(nodes.shape[2]):
        value = float(WEIGHTS[1]) * nodes[0, 1, z]
        for j in range(2, NODES):
            value = value + float(WEIGHTS[j]) * nodes[0, j, z]
        weighted[z] = value + (first * float(WEIGHTS[0])) * nodes[0, 0, z]
        cells = kappa_of(labels[z], table)
        total = cells if z == 0 else total + cells
    block[...] = total
    kappa[0] = pair_mean(block)


def weigh(info, table, node_fields, labels):
    _, _, nz, nx, ny = node_fields.shape
    cut = 4
    return pl.pallas_call(
        weigh_kernel,
        grid=(nz // cut,),
        in_specs=[
            SMEM, SMEM,
            pl.BlockSpec((1, NODES, cut, nx, ny), lambda i: (0, 0, i, 0, 0)),
            pl.BlockSpec((cut, nx, ny), lambda i: (i, 0, 0)),
        ],
        out_specs=[
            pl.BlockSpec((cut, nx, ny), lambda i: (i, 0, 0)),
            pl.BlockSpec((1, nx // 2, ny), lambda i: (i, 0, 0)),
        ],
        out_shape=[
            jax.ShapeDtypeStruct((nz, nx, ny), F32),
            jax.ShapeDtypeStruct((nz // 4, nx // 2, ny), F32),
        ],
        scratch_shapes=[pltpu.VMEM((nx, ny), F32)],
        compiler_params=pltpu.CompilerParams(vmem_limit_bytes=16 * MIB),
        name="weigh",
    )(info, table, node_fields, labels)


def residual_kernel(
    info, table, weighted, arrived, u0, u4, labels, label_low, label_high, shift, cells,
    coarse, start, wide, block,
):
    nz, nx, ny = weighted.shape
    first = info[0] == 0
    advect = shift[...].astype(F32)
    w0 = float(WEIGHTS[0])
    blank = jnp.zeros((nx, ny), F32)
    wide[0, pl.ds(8, nx)] = blank
    wide[nz + 1, pl.ds(8, nx)] = blank
    for z in range(nz):
        put_ring(wide, z + 1, weighted[z] + w0 * arrived[z])
    for zb in range(nz // 4):
        total = None
        for k in range(4):
            z = 4 * zb + k
            begin = jnp.where(first, u0[0, 0, z], arrived[z])
            start[z] = begin
            value = begin - u4[0, 0, z] + rate(
                wide[z, pl.ds(8, nx)], wide[z + 1, pl.ds(8, nx)], wide[z + 2, pl.ds(8, nx)],
                wide[z + 1, pl.ds(7, nx)], wide[z + 1, pl.ds(9, nx)],
                kappa_of(labels[z], table), advect,
            )
            total = value if total is None else total + value
        block[...] = total
        coarse[zb] = pair_mean(block)
    block[...] = kappa_of(label_low[nz - 1], table) * wide[1, pl.ds(8, nx)]
    coarse[nz // 4] = pair_mean(block)
    block[...] = kappa_of(label_high[0], table) * wide[nz, pl.ds(8, nx)]
    coarse[nz // 4 + 1] = pair_mean(block)
    coarse[nz // 4 + 2] = cells[0]
    coarse[nz // 4 + 3] = cells[1]


def residual(
    info, table, weighted, arrived, node_fields, labels, label_low, label_high, shift, cells
):
    nz, nx, ny = weighted.shape
    slab = whole((nz, nx, ny))
    return pl.pallas_call(
        residual_kernel,
        grid=(1,),
        in_specs=[
            SMEM, SMEM, slab, slab, node_block(0, nz, nx, ny), node_block(NODES - 1, nz, nx, ny),
            slab, slab, slab, whole((1, ny)), whole(cells.shape),
        ],
        out_specs=[whole((nz // 4 + 4, nx // 2, ny)), slab],
        out_shape=[
            jax.ShapeDtypeStruct((nz // 4 + 4, nx // 2, ny), F32),
            jax.ShapeDtypeStruct((nz, nx, ny), F32),
        ],
        scratch_shapes=[pltpu.VMEM((nz + 2, nx + 16, ny), F32), pltpu.VMEM((nx, ny), F32)],
        compiler_params=pltpu.CompilerParams(vmem_limit_bytes=20 * MIB),
        name="residual",
    )(
        info, table, weighted, arrived, node_fields, node_fields, labels, label_low, label_high,
        shift, cells,
    )


def pack_kernel(nodes, start, packed):
    for z in range(nodes.shape[2]):
        u = [start[z]] + [nodes[0, j, z] for j in range(1, NODES)]
        for m in range(STEPS):
            coef = [float(Q[m, j]) for j in range(NODES)]
            if m > 0:
                coef[m] -= float(DT[m])
            total = coef[0] * u[0]
            for j in range(1, NODES):
                total = total + coef[j] * u[j]
            packed[m, z] = total
        packed[STEPS, z] = u[0]


def pack(node_fields, start):
    _, _, nz, nx, ny = node_fields.shape
    cut = 2
    return pl.pallas_call(
        pack_kernel,
        grid=(nz // cut,),
        in_specs=[
            pl.BlockSpec((1, NODES, cut, nx, ny), lambda i: (0, 0, i, 0, 0)),
            pl.BlockSpec((cut, nx, ny), lambda i: (i, 0, 0)),
        ],
        out_specs=pl.BlockSpec((NODES, cut, nx, ny), lambda i: (0, i, 0, 0)),
        out_shape=jax.ShapeDtypeStruct((NODES, nz, nx, ny), F32),
        compiler_params=pltpu.CompilerParams(vmem_limit_bytes=16 * MIB),
        name="pack",
    )(node_fields, start)


def coarse_step(src, dst, kappa, half):
    nz, nx, ny = kappa.shape
    lane = lax.broadcasted_iota(jnp.int32, (8, ny), 1)
    for x in range(0, nx, 8):
        rows = pl.ds(8 + x, 8)
        below, mid = src[0, rows], src[1, rows]
        for z in range(nz):
            above = src[z + 2, rows]
            past = src[z + 1, pl.ds(7 + x, 8)]
            ahead = src[z + 1, pl.ds(9 + x, 8)]
            left = jnp.where(lane == 0, 0.0, pltpu.roll(mid, 1, 1))
            right = jnp.where(lane == ny - 1, 0.0, pltpu.roll(mid, ny - 1, 1))
            total = (below + above) * 0.0625 + (past + ahead) * 0.25 + ((left + right) - 2.625 * mid)
            value = mid + kappa[z, pl.ds(x, 8)] * total - half * (mid - past)
            dst[z + 1, rows] = value
            if x == 0:
                dst[z + 1, 8 + nx : 9 + nx] = value[0:1]
            if x == nx - 8:
                dst[z + 1, 7:8] = value[7:8]
            below, mid = mid, above


def clear_edges(*buffers):
    for ref in buffers:
        nz, nx = ref.shape[0] - 2, ref.shape[1] - 16
        blank = jnp.zeros((nx, ref.shape[2]), F32)
        ref[0, pl.ds(8, nx)] = blank
        ref[nz + 1, pl.ds(8, nx)] = blank


def get_layer(state, z):
    return state[z + 1, pl.ds(8, state.shape[1] - 16)]


def add_layers(state, member, nz):
    for z in range(nz):
        put_ring(state, z + 1, get_layer(state, z) + member[z])


def entry_kernel(info, gathered, shift, field, kappa, packet):
    ns, parts, nx, ny = gathered.shape
    for s in range(ns):
        low = gathered[s, 0]
        high = gathered[s, 1]
        if s > 0:
            low = low + gathered[s - 1, 3]
        if s < ns - 1:
            high = high + gathered[s + 1, 2]
        field[2 * s] = low
        field[2 * s + 1] = high
        kappa[2 * s] = gathered[s, 4]
        kappa[2 * s + 1] = gathered[s, 5]
    core = info[4] % 2
    for k in range(ns):
        packet[pl.ds(k * nx, nx)] = field[core * ns + k]
    packet[pl.ds(ns * nx, 8)] = jnp.broadcast_to(shift[...].astype(F32) * 0.5, (8, ny))


def chain_entry(info, gathered, shift):
    ns, _, nx, ny = gathered.shape
    return pl.pallas_call(
        entry_kernel,
        in_specs=[SMEM, VMEM, VMEM],
        out_specs=[VMEM] * 3,
        out_shape=[
            jax.ShapeDtypeStruct((2 * ns, nx, ny), F32),
            jax.ShapeDtypeStruct((2 * ns, nx, ny), F32),
            jax.ShapeDtypeStruct((ns * nx + 8, ny), F32),
        ],
        compiler_params=pltpu.CompilerParams(vmem_limit_bytes=8 * MIB),
        name="chain_entry",
    )(info, gathered, shift)


def place(members, slot, core, mine, theirs):
    _, nz, nx, _ = members.shape
    half = nz // 2
    for k in range(half):
        members[slot, core * half + k] = mine[pl.ds(k * nx, nx)]
        members[slot, (1 - core) * half + k] = theirs[pl.ds(k * nx, nx)]


def halves_of(halves, base, ref, row, count):
    for j in range(count):
        halves[base + j] = jnp.broadcast_to(ref[row + j : row + j + 1], halves.shape[1:])


def level_kernel(length, axis, info, own, tail, before, kappa, *refs):
    packets, (packet, full, after, members, halves, ping, pong, saved) = refs[:6], refs[6:]
    nz, nx, ny = kappa.shape
    core, position = info[4] % 2, info[axis]
    inner = info[3] if length > 1 else 0
    base = nz // 2 * nx
    for z in range(nz):
        members[position, z] = own[z]
    halves_of(halves, position * length, tail, base, length)
    for k in range(1, 4):
        slot = (position + (4 - k)) % 4
        mine, theirs = packets[2 * (k - 1)], packets[2 * (k - 1) + 1]
        place(members, slot, core, mine, theirs)
        halves_of(halves, slot * length, mine, base, length)
    clear_edges(ping, pong)
    for z in range(nz):
        put_ring(ping, z + 1, members[0, z])
    saved[...] = jnp.zeros(saved.shape, F32)

    def member(group, here, there):
        for j in range(length):
            @pl.when((group == position) & (j == inner))
            def _(here=here):
                for z in range(nz):
                    saved[z] = get_layer(here, z)

            coarse_step(here, there, kappa, halves[group * length + j])
            here, there = there, here
        add_layers(here, members.at[group], nz)
        return here

    if length % 2:
        last, other = ping, pong
        for group in range(1, 4):
            last, other = member(group, last, other), last
    else:
        lax.fori_loop(1, 4, lambda group, _: (member(group, ping, pong), 0)[1], 0)
        last = ping
    after[...] = saved[...] + before[...] if length > 1 else saved[...]
    for z in range(nz):
        full[z] = get_layer(last, z)
    for k in range(nz // 2):
        packet[pl.ds(k * nx, nx)] = full[core * (nz // 2) + k]
    for j in range(4 * length):
        packet[base + j : base + j + 1] = halves[j, 0:1]
    if length == 1:
        packet[base + 4 : base + 8] = halves[0, 0:4]


def chain_level(length, axis, info, own, tail, before, kappa, packets):
    nz, nx, ny = kappa.shape
    return pl.pallas_call(
        functools.partial(level_kernel, length, axis),
        in_specs=[SMEM] + [VMEM] * (4 + len(packets)),
        out_specs=[VMEM] * 3,
        out_shape=[
            jax.ShapeDtypeStruct((nz // 2 * nx + max(8, 4 * length), ny), F32),
            jax.ShapeDtypeStruct((nz, nx, ny), F32),
            jax.ShapeDtypeStruct((nz, nx, ny), F32),
        ],
        scratch_shapes=[
            pltpu.VMEM((4, nz, nx, ny), F32),
            pltpu.VMEM((4 * length, 8, ny), F32),
            pltpu.VMEM((nz + 2, nx + 16, ny), F32),
            pltpu.VMEM((nz + 2, nx + 16, ny), F32),
            pltpu.VMEM((nz, nx, ny), F32),
        ],
        compiler_params=pltpu.CompilerParams(vmem_limit_bytes=12 * MIB),
        name=f"chain_level_{length}",
    )(info, own, tail, before, kappa, *packets)


def finish_chain(info, field, tail, before, kappa, packets, coarse, members, halves, ping, pong):
    nz, nx, ny = kappa.shape
    core, zh = info[4] % 2, info[1]
    inside = info[2] * 4 + info[3]
    base = nz // 2 * nx
    halves_of(halves, zh * 16, tail, base, 16)
    for k in range(1, 4):
        slot = (zh + (4 - k)) % 4
        mine, theirs = packets[2 * (k - 1)], packets[2 * (k - 1) + 1]
        place(members, slot, core, mine, theirs)
        halves_of(halves, slot * 16, mine, base, 16)
    begin = zh * 16
    clear_edges(ping, pong)
    for z in range(nz):
        put_ring(ping, z + 1, jnp.where(zh > 0, members[0, z], 0.0))

    def pair(t, _):
        coarse_step(ping, pong, kappa, halves[2 * t])
        coarse_step(pong, ping, kappa, halves[2 * t + 1])
        return 0

    def group(g, _):
        lax.fori_loop(0, 8, lambda i, _: pair(8 * g + i, 0), 0, unroll=4)
        add_layers(ping, members.at[g], nz)
        return 0

    lax.fori_loop(1, zh, group, 0)

    @pl.when(zh > 0)
    def _():
        lax.fori_loop(8 * zh, 8 * zh + inside // 2, pair, 0)

        @pl.when(inside % 2 == 1)
        def _():
            coarse_step(ping, pong, kappa, halves[begin + inside - 1])
            for z in range(nz):
                put_ring(ping, z + 1, get_layer(pong, z))

    add_layers(ping, before, nz)
    coarse_step(ping, pong, kappa, halves[begin + inside])
    blank = jnp.zeros((nx, ny), F32)
    for f in range(2):
        for edge in range(2):
            coarse[f, edge] = blank
            coarse[f, nz + 2 + edge] = blank
    for z in range(nz):
        value = get_layer(ping, z)
        coarse[0, z + 2] = value
        coarse[1, z + 2] = get_layer(pong, z) + field[z] - value


CHUNK = 32


def sweeps_kernel(
    info, table, own, low, high, labels, labels_low, labels_high, shift,
    field, tail, before, kappa_c, p0, p1, p2, p3, p4, p5, out,
    coarse, members, halves, ping, pong, held, marks, lift, kappa, first, mixed_a, mixed_b, *rest,
):
    fields, second, (sems, out_sems) = rest[:STEPS], rest[STEPS : 2 * STEPS], rest[2 * STEPS :]
    mixed = (mixed_a, mixed_b)
    nz, nx, ny = labels.shape
    wide = 3 * nz
    space = info[4]
    copies = []
    for k, (src, mark) in enumerate(((low, labels_low), (own, labels), (high, labels_high))):
        copies.append(
            pltpu.make_async_copy(mark, marks.at[pl.ds(k * nz, nz)], sems.at[2 * k])
        )
        copies.append(
            pltpu.make_async_copy(src, held.at[:, pl.ds(k * nz, nz)], sems.at[2 * k + 1])
        )
    for copy in copies:
        copy.start()
    finish_chain(
        info, field, tail, before, kappa_c, (p0, p1, p2, p3, p4, p5), coarse, members, halves, ping, pong
    )
    advect = jnp.broadcast_to(shift[...].astype(F32), (CHUNK, ny))
    for f in range(2):
        for k in range(wide // 4):
            value = coarse[f, space * (nz // 4) + k]
            lift[f, k, pl.ds(0, nx // 2, stride=2), :] = value
            lift[f, k, pl.ds(1, nx // 2, stride=2), :] = value
    for copy in copies:
        copy.wait()

    def layers(low, high, body):
        lax.fori_loop(low, high, lambda z, _: (body(z), 0)[1], 0, unroll=True)

    def mix(slot, z, c, value):
        ref = mixed[slot]
        ref[z, pl.ds(8 + c, CHUNK)] = value
        if c == 0:
            ref[z, 8 + nx : 9 + nx] = value[0:1]
        if c == nx - CHUNK:
            ref[z, 7:8] = value[CHUNK - 1 : CHUNK]

    def opening(z):
        inside = ((z >= nz) | (space > 0)) & ((z < 2 * nz) | (space < 3))
        at = z // 4
        for c in range(0, nx, CHUNK):
            rows = pl.ds(c, CHUNK)
            kappa[z, rows] = jnp.where(inside, kappa_of(marks[z, rows], table), 0.0)
            begin, grow = lift[0, at, rows], lift[1, at, rows]
            first[z, rows] = held[STEPS, z, rows] + begin
            value = held[0, z, rows] + float(DT[0]) * begin + float(0.5 * DT[0] ** 2) * grow
            mix(0, z, c, value)

    layers(0, wide, opening)

    def later_sum(m, z, rows, newest):
        total = None
        for j in range(NODES):
            coef = float(Q[m, j] - (DT[m] if m == j else 0.0))
            node = first[z, rows] if j == 0 else fields[j - 1][z, rows]
            if j == NODES - 1 and newest is not None:
                node = newest
            total = coef * node if total is None else total + coef * node
        return total

    outs = [pltpu.make_async_copy(first.at[pl.ds(nz, nz)], out.at[0, 0], out_sems.at[0])]
    outs[0].start()
    for turn in range(2 * STEPS):
        sweep, m = turn // STEPS, turn % STEPS
        past = first if m == 0 else (fields if sweep == 0 else second)[m - 1]
        target = (fields if sweep == 0 else second)[m]
        now, later = turn % 2, (turn + 1) % 2

        def stage(z, turn=turn, sweep=sweep, m=m, past=past, target=target, now=now, later=later):
            source = mixed[now]
            for c in range(0, nx, CHUNK):
                rows, inner = pl.ds(c, CHUNK), pl.ds(8 + c, CHUNK)
                value = past[z, rows] + rate(
                    source[z - 1, inner], source[z, inner], source[z + 1, inner],
                    source[z, pl.ds(7 + c, CHUNK)], source[z, pl.ds(9 + c, CHUNK)],
                    kappa[z, rows], advect,
                )
                target[z, rows] = value
                if turn == 2 * STEPS - 1:
                    continue
                if turn < STEPS - 1:
                    blend = (
                        float(DT[m + 1]) * value
                        + held[m + 1, z, rows]
                        + float(0.5 * DT[m + 1] ** 2) * lift[1, z // 4, rows]
                    )
                elif turn == STEPS - 1:
                    blend = later_sum(0, z, rows, value) + float(DT[0]) * first[z, rows]
                else:
                    blend = later_sum(m + 1, z, rows, None) + float(DT[m + 1]) * value
                mix(later, z, c, blend)

        layers(turn + 1, wide - 1 - turn, stage)
        if sweep == 1:
            copy = pltpu.make_async_copy(
                target.at[pl.ds(nz, nz)], out.at[0, m + 1], out_sems.at[m + 1]
            )
            copy.start()
            outs.append(copy)
    for copy in outs:
        copy.wait()


def fine_sweeps(info, table, fine, chain):
    nz, nx, ny = fine[3].shape
    nzc, nxc, _ = chain[3].shape
    wide = 3 * nz
    return pl.pallas_call(
        sweeps_kernel,
        in_specs=[SMEM, SMEM] + [ANY] * 6 + [VMEM] * 11,
        out_specs=ANY,
        out_shape=jax.ShapeDtypeStruct((1, NODES, nz, nx, ny), F32),
        scratch_shapes=[
            pltpu.VMEM((2, nzc + 4, nxc, ny), F32),
            pltpu.VMEM((4, nzc, nxc, ny), F32),
            pltpu.VMEM((64, 8, ny), F32),
            pltpu.VMEM((nzc + 2, nxc + 16, ny), F32),
            pltpu.VMEM((nzc + 2, nxc + 16, ny), F32),
            pltpu.VMEM((NODES, wide, nx, ny), F32),
            pltpu.VMEM((wide, nx, ny), jnp.int32),
            pltpu.VMEM((2, wide // 4, nx, ny), F32),
            pltpu.VMEM((wide, nx, ny), F32),
            pltpu.VMEM((wide, nx, ny), F32),
            pltpu.VMEM((wide, nx + 16, ny), F32),
            pltpu.VMEM((wide, nx + 16, ny), F32),
        ]
        + [pltpu.VMEM((wide, nx, ny), F32)] * (2 * STEPS)
        + [
            pltpu.SemaphoreType.DMA((6,)),
            pltpu.SemaphoreType.DMA((NODES,)),
        ],
        compiler_params=pltpu.CompilerParams(vmem_limit_bytes=40 * MIB),
        name="fine_sweeps",
    )(info, table, *fine, *chain)


def to_space(value, by):
    return lax.ppermute(value, "space", [(i, i + by) for i in range(4) if 0 <= i + by < 4])


def to_next(value, by):
    axes = TM + ("space",)
    pairs = [
        (4 * n + s, 4 * (n + 1) + s + by) for n in range(63) for s in range(4) if 0 <= s + by < 4
    ]
    return lax.ppermute(value, axes, pairs)


def swap_core(value):
    return lax.ppermute(value, "space", [(0, 1), (1, 0), (2, 3), (3, 2)])


def gather_axis(packet, axis, cyclic=True):
    packets = []
    for k in range(1, 4):
        pairs = [(i, (i + k) % 4) for i in range(4) if cyclic or i + k < 4]
        got = lax.ppermute(packet, axis, pairs)
        packets += [got, swap_core(got)]
    return packets


def shards(node_fields, region_label, sheet_shift, diffusivity):
    zh, y, x = (lax.axis_index(a) for a in TM)
    space = lax.axis_index("space")
    info = jnp.stack([zh * 16 + y * 4 + x, zh, y, x, space]).astype(jnp.int32)
    arrived = to_next(node_fields[0, NODES - 1], 0)
    labels_low, labels_high = to_space(region_label, 1), to_space(region_label, -1)
    weighted, cells = weigh(info, diffusivity, node_fields, region_label)
    coarse, start = residual(
        info, diffusivity, weighted, arrived, node_fields, region_label, labels_low, labels_high,
        sheet_shift, cells,
    )
    gathered = lax.all_gather(coarse, "space", axis=0, tiled=False)
    field, kappa, packet = chain_entry(info, gathered, sheet_shift)
    packets = gather_axis(packet, "x")
    start, _ = lax.optimization_barrier((start, packet))
    packed = pack(node_fields, start)
    packed, packets[4] = lax.optimization_barrier((packed, packets[4]))
    packed_low, packed_high = to_space(packed, 1), to_space(packed, -1)
    packet, field4, prefix = chain_level(1, 3, info, field, packet, field, kappa, packets)
    packets = gather_axis(packet, "y")
    packet, _, prefix = chain_level(4, 2, info, field4, packet, prefix, kappa, packets)
    packets = gather_axis(packet, "zh", False)
    return fine_sweeps(
        info,
        diffusivity,
        (packed, packed_low, packed_high, region_label, labels_low, labels_high, sheet_shift),
        (field, packet, prefix, kappa, *packets),
    )


def solution(mesh):
    grid = Mesh(mesh.devices.reshape(4, 4, 4, 4), TM + ("space",))
    in_specs = (P(TM, None, "space", None, None), P("space", None, None), P(TM, None), P())
    out_specs = P(TM, None, "space", None, None)
    return jax.shard_map(shards, mesh=grid, in_specs=in_specs, out_specs=out_specs, check_vma=False)
```
